512 devices in a mesh: tp: 16 (over y_hi, z), sq: 8 (over x, core), sg: 4 (over y_lo).
Axes of the slice: x: 4, y: 8 (y_hi: 2, y_lo: 4; y = y_hi * 4 + y_lo), z: 8, core: 2. Of those that a mesh axis runs over, the one named last changes fastest.
Arguments:
- query: float32 [4, 1024, 4096], P('sg', 'sq', 'tp'), may hold values from -5 to 5
- key_in: float32 [4, 1024, 4096], P('sg', 'sq', 'tp'), may hold values from -5 to 5
- value: float32 [4, 1024, 4096], P('sg', 'sq', 'tp'), may hold values from -6 to 6
- out_grad: float32 [4, 1024, 4096], P('sg', 'sq', 'tp'), may hold values from -4 to 4
- w_out: float32 [4096, 4096], P(('sq', 'sg'), 'tp'), may hold values from -0.09375 to 0.09375
Outputs:
- query_grad: float32 [4, 1024, 4096], P('sg', 'sq', 'tp')
- key_grad: float32 [4, 1024, 4096], P('sg', 'sq', 'tp')
- value_grad: float32 [4, 1024, 4096], P('sg', 'sq', 'tp')
- w_out_grad: float32 [4096, 4096], P(('sq', 'sg'), 'tp')
The draws below stay inside these ranges and needn't reach their ends.
All inputs are finite; a program needn't handle non-finite values.
Results may differ from the reference program's by a relative error of at most 0.00095.
Values sent between devices are 32-bit elements; how exact they have to be, the bound alone decides.
A program may use at most 64 MiB of HBM per device.

```python
import math
import jax
import jax.numpy as jnp
from jax import lax

D = 4096
HEADS = 32
HDIM = 128
SEG_LEN = 1024
SEGS = 4


def sign_pattern(key):
    return jax.random.rademacher(key, (SEGS, SEG_LEN, HEADS * HDIM), dtype=jnp.float32)


def draw_query(key, part):
    sign_table = sign_pattern(key)
    key = jax.random.fold_in(key, 1)
    sampled = jax.random.truncated_normal(key, -5.0, 5.0, sign_table.shape, jnp.float32)
    return sampled


def draw_key_in(key, part):
    sign_table = sign_pattern(key)
    key = jax.random.fold_in(key, 2)
    sampled = jax.random.truncated_normal(key, -5.0, 5.0, sign_table.shape, jnp.float32)
    return sampled


def level_of(rng, extent, split, low, top_value):
    def one(dim, blocks):
        heights = jax.random.uniform(jax.random.fold_in(jax.random.fold_in(rng, 6), dim), (blocks,), jnp.float32, low / len(split), top_value / len(split))
        return jnp.repeat(jnp.exp(heights), extent[dim] // blocks).reshape((-1,) + (1,) * (len(extent) - dim - 1))

    gain = one(*split[0])
    for cut in split[1:]:
        gain = gain * one(*cut)
    return gain


def noise(own_key, dims, deviation, limit, cuts=(), kind=jnp.bfloat16):
    values = jax.random.normal(own_key, dims, jnp.float32) * deviation
    if len(cuts) > 0:
        values = level_of(own_key, dims, cuts, -0.22, 0.18) * values
    return jnp.clip(values, min=-limit, max=limit).astype(kind)


def setup_inputs(seed: int = 0) -> dict:
    arg_keys = jax.random.split(jax.random.key(seed), 6)
    query = draw_query(jax.random.fold_in(arg_keys[5], 71), 0)
    key_in = draw_key_in(jax.random.fold_in(arg_keys[5], 71), 0)
    value = noise(arg_keys[2], (SEGS, SEG_LEN, HEADS * HDIM), 1.0, 6.0, ((0, 4), (1, 8), (2, 16)), jnp.float32)
    out_grad = noise(arg_keys[3], (SEGS, SEG_LEN, D), 0.5, 4.0, ((0, 4), (1, 8), (2, 16)), jnp.float32)
    w_out = noise(arg_keys[4], (D, HEADS * HDIM), (HEADS * HDIM) ** -0.5, 0.09375, ((0, 32), (1, 16)), jnp.float32)
    return dict(query=query, key_in=key_in, value=value, out_grad=out_grad, w_out=w_out)


def reference(query, key_in, value, out_grad, w_out):
    highest = lax.Precision.HIGHEST
    scale_inv = 1.0 / math.sqrt(HDIM)
    feat_width = HEADS * HDIM

    def segment_backward(segment):
        queries, keys_seg, values_seg, grad_seg = segment
        q_heads = queries.reshape(SEG_LEN, HEADS, HDIM)
        k_heads = keys_seg.reshape(SEG_LEN, HEADS, HDIM)
        v_heads = values_seg.reshape(SEG_LEN, HEADS, HDIM)
        scores = jnp.einsum('thd,shd->hts', q_heads, k_heads, precision=highest) * scale_inv
        row_top = lax.optimization_barrier(jnp.max(scores, axis=2, keepdims=True))
        expos = jnp.exp(scores - row_top)
        probs = expos / lax.optimization_barrier(jnp.sum(expos, axis=2, keepdims=True))
        attended = jnp.einsum('hts,shd->thd', probs, v_heads, precision=highest)
        d_attended = jnp.dot(grad_seg, w_out, precision=highest).reshape(SEG_LEN, HEADS, HDIM)
        delta_rows = lax.optimization_barrier(jnp.sum(d_attended * attended, axis=2)).T
        d_probs = jnp.einsum('thd,shd->hts', d_attended, v_heads, precision=highest)
        d_scores = probs * (d_probs - delta_rows[:, :, None])
        grad_q = jnp.einsum('hts,shd->thd', d_scores, k_heads, precision=highest) * scale_inv
        grad_k = jnp.einsum('hts,thd->shd', d_scores, q_heads, precision=highest) * scale_inv
        grad_v = jnp.einsum('hts,thd->shd', probs, d_attended, precision=highest)
        weight_part = jnp.dot(grad_seg.T, attended.reshape(SEG_LEN, feat_width), precision=highest)
        return (grad_q.reshape(SEG_LEN, feat_width), grad_k.reshape(SEG_LEN, feat_width), grad_v.reshape(SEG_LEN, feat_width), weight_part)
    grads_q, grads_k, grads_v, weight_parts = lax.map(segment_backward, (query, key_in, value, out_grad))
    return (grads_q, grads_k, grads_v, lax.optimization_barrier(jnp.sum(weight_parts, axis=0)))
```

```python
import math

import jax
import jax.numpy as jnp
from jax import lax
from jax.experimental import pallas as pl
from jax.experimental.pallas import tpu as pltpu
from jax.sharding import PartitionSpec as P

HD = 128
F32 = jnp.float32
BF16 = jnp.bfloat16
NN = (((1,), (0,)), ((), ()))
NT = (((1,), (1,)), ((), ()))
TN = (((0,), (0,)), ((), ()))


def rcopy(src, dst, ssem, rsem, **dev):
    return pltpu.make_async_remote_copy(
        src_ref=src,
        dst_ref=dst,
        send_sem=ssem,
        recv_sem=rsem,
        device_id=dev,
        device_id_type=pl.DeviceIdType.MESH,
    )


def split(x):
    hi = x.astype(BF16)
    return hi, (x - hi.astype(F32)).astype(BF16)


def dot3(a, b, dims):
    d = lambda u, v: lax.dot_general(u, v, dims, preferred_element_type=F32)
    return d(a[0], b[0]) + (d(a[0], b[1]) + d(a[1], b[0]))


def body(
    q_ref, k_ref, v_ref, og_ref, w_ref,
    dq_ref, dk_ref, dv_ref, dw_ref,
    kvw, ogb, oghi, oglo, att, psend, dpart, part, sib, red, half, full,
    khi, klo, vhi, vlo, whi, wlo, pt, phi, plo,
    xs, xr, ss, sr, ys, yr, zs, zo, zr, ts, tr, ds, dr, rs1, rr1, rs2, rr2,
):
    t = lax.axis_index("tp")
    q = lax.axis_index("sq")
    s = lax.axis_index("sg")
    yh, z = lax.div(t, 8), lax.rem(t, 8)
    x, c = lax.div(q, 2), lax.rem(q, 2)
    par = lax.div(s, 2)
    odd = lax.rem(z + par, 2)
    ring = lambda d: yh * 8 + lax.rem(z + d + 8, 8)
    sq_at = lambda d: lax.rem(q + 2 * d + 8, 8)
    q_right, q_left, q_far, q_sib = sq_at(1), sq_at(-1), sq_at(2), x * 2 + 1 - c
    sibling = lambda b: b + 1 - 2 * c
    seg_at = lambda k: lax.rem(s + 1 + k, 4)

    barrier = pltpu.get_barrier_semaphore()
    partners = [{"sq": q_sib}, {"sq": q_right}, {"sq": q_left}, {"tp": ring(1)}, {"tp": ring(-1)}]
    for d in range(4):
        partners.append({"tp": (1 - yh) * 8 + z, "sg": lax.rem(s + d, 4)})
        if d > 0:
            partners.append({"sg": lax.rem(s + d, 4)})
    for p in partners:
        pl.semaphore_signal(barrier, inc=1, device_id=p, device_id_type=pl.DeviceIdType.MESH)
    pl.semaphore_wait(barrier, len(partners))

    sends = []

    def go(copy):
        copy.start()
        sends.append(copy)

    zi_own = lax.div(z, 2)
    ysend = []
    for h in range(2):
        target = 2 * lax.rem(z, 2) + h
        for y in range(2):
            mine = jnp.logical_and(yh == y, s == target)
            cp = rcopy(
                og_ref.at[:, pl.ds(h * HD, HD)],
                ogb.at[zi_own, s, yh],
                ys.at[h, y],
                yr.at[s, yh],
                tp=y * 8 + z,
                sg=target,
            )
            ysend.append((mine, cp))

            @pl.when(jnp.logical_not(mine))
            def _():
                cp.start()

            @pl.when(mine)
            def _():
                ogb[zi_own, s, yh] = og_ref[:, pl.ds(h * HD, HD)]

    ins = (k_ref, v_ref, w_ref)
    for a in range(3):
        go(rcopy(ins[a], kvw.at[a, q], xs.at[a, 0], xr.at[a, 0], sq=q_right))
        go(rcopy(ins[a], kvw.at[a, q], xs.at[a, 1], xr.at[a, 1], sq=q_left))
        go(rcopy(ins[a], kvw.at[a, q], ss.at[a, 0], sr.at[a, 0], sq=q_sib))
    for a in range(3):
        kvw[a, q] = ins[a][...]

    def near(a):
        rcopy(ins[a], kvw.at[a, q_left], xs.at[a, 0], xr.at[a, 0], sq=q_right).wait_recv()
        up = kvw.at[a, q_left, pl.ds(0, 64)]
        go(rcopy(up, up, xs.at[a, 2], xr.at[a, 2], sq=q_right))
        blk = kvw.at[a, q_left]
        go(rcopy(blk, blk, ss.at[a, 1], sr.at[a, 1], sq=q_sib))
        rcopy(ins[a], kvw.at[a, q_right], xs.at[a, 1], xr.at[a, 1], sq=q_left).wait_recv()
        low = kvw.at[a, q_right, pl.ds(64, 64)]
        go(rcopy(low, low, xs.at[a, 3], xr.at[a, 3], sq=q_left))
        blk = kvw.at[a, q_right]
        go(rcopy(blk, blk, ss.at[a, 2], sr.at[a, 2], sq=q_sib))

    def far(a):
        up = kvw.at[a, q_far, pl.ds(0, 64)]
        rcopy(up, up, xs.at[a, 2], xr.at[a, 2], sq=q_right).wait_recv()
        low = kvw.at[a, q_far, pl.ds(64, 64)]
        rcopy(low, low, xs.at[a, 3], xr.at[a, 3], sq=q_left).wait_recv()
        blk = kvw.at[a, q_far]
        go(rcopy(blk, blk, ss.at[a, 3], sr.at[a, 3], sq=q_sib))

    def siblings(a):
        for i, b in enumerate((q, q_left, q_right, q_far)):
            blk = kvw.at[a, sibling(b)]
            rcopy(blk, blk, ss.at[a, i], sr.at[a, i], sq=q_sib).wait_recv()

    def chunk(d, k):
        zi = lax.div(lax.rem(z - d + 16, 8), 2)
        return ogb.at[zi, seg_at(k)], zr.at[k, zi]

    def zcopy(d, k, sem, step):
        ref, rsem = chunk(d, k)
        return rcopy(ref, ref, sem, rsem, tp=ring(step))

    def own(k):
        @pl.when(odd == 0)
        def _():
            j = seg_at(k)
            for y in range(2):
                @pl.when(jnp.logical_not(jnp.logical_and(j == s, yh == y)))
                def _():
                    blk = ogb.at[zi_own, j, y]
                    rcopy(blk, blk, ys.at[0, y], yr.at[j, y], tp=t, sg=s).wait_recv()
            zcopy(0, k, zo.at[k, 0], 1).start()
            zcopy(0, k, zo.at[k, 1], -1).start()

    def pass_near(k):
        cp = zcopy(2 - odd, k, zs.at[k, 0], 1)
        cp.wait_recv()
        go(cp)
        cp = zcopy(6 + odd, k, zs.at[k, 1], -1)
        cp.wait_recv()
        go(cp)

    def pass_far(k):
        right_longer = k % 2 == 0
        cp = zcopy(4 - odd, k, zs.at[k, 2], 1 if right_longer else -1)
        cp.wait_recv()
        if right_longer:
            @pl.when(odd == 1)
            def _():
                cp.start()
                zcopy(5, k, zs.at[k, 2], -1).wait_recv()
        else:
            @pl.when(odd == 1)
            def _():
                cp2 = zcopy(5, k, zs.at[k, 2], -1)
                cp2.wait_recv()
                cp2.start()

    def partial_dot(k):
        j = seg_at(k)
        for zi in range(4):
            for y in range(2):
                hi, lo = split(ogb[zi, j, y])
                cols = pl.ds((y * 4 + zi) * HD, HD)
                oghi[j, :, cols] = hi
                oglo[j, :, cols] = lo
        res = dot3((oghi[j], oglo[j]), (whi[...], wlo[...]), NN)
        psend[k] = res
        if k < 3:
            go(rcopy(psend.at[k], dpart.at[k], ds.at[k], dr.at[k], sg=j))

    own(0)
    own(1)
    near(0)
    near(1)
    far(0)
    near(2)
    pass_near(0)
    own(2)
    far(1)
    far(2)
    pass_far(0)

    qs = q_ref[...] * (1.0 / math.sqrt(HD))
    qsp = [split(qs[:, h * HD:(h + 1) * HD]) for h in range(2)]
    siblings(0)
    for b in range(8):
        rows = pl.ds(b * 128, 128)
        khi[rows, :], klo[rows, :] = split(kvw[0, b])
    for h in range(2):
        cols = pl.ds(h * HD, HD)
        st = dot3((khi[:, cols], klo[:, cols]), qsp[h], NT)
        e = jnp.exp(st - jnp.max(st, axis=0, keepdims=True))
        p = e / jnp.sum(e, axis=0, keepdims=True)
        pt[h] = p
        phi[h], plo[h] = split(p)

    pass_near(1)
    own(3)
    siblings(1)
    for b in range(8):
        rows = pl.ds(b * 128, 128)
        vhi[rows, :], vlo[rows, :] = split(kvw[1, b])
    for h in range(2):
        cols = pl.ds(h * HD, HD)
        att[s, :, cols] = dot3((phi[h], plo[h]), (vhi[:, cols], vlo[:, cols]), TN)
    for k in range(3):
        go(rcopy(att.at[s], att.at[s], ts.at[k], tr.at[k], sg=seg_at(k)))
    pass_far(1)
    siblings(2)
    for b in range(8):
        rows = pl.ds(b * 128, 128)
        whi[rows, :], wlo[rows, :] = split(kvw[2, b])
    pass_near(2)
    partial_dot(0)
    partial_dot(1)
    pass_far(2)
    pass_near(3)
    partial_dot(2)
    pass_far(3)
    partial_dot(3)

    outs = (dk_ref, dv_ref, dw_ref)
    x_right, x_left, x_far = lax.rem(x + 1, 4), lax.rem(x + 3, 4), lax.rem(x + 2, 4)
    half_up, half_low = pl.ds(0, 64), pl.ds(64, 64)

    def put(a, val, cols):
        for b in range(8):
            part[a, b // 2, b % 2, :, cols] = val[b * 128:(b + 1) * 128]

    def sum_start(a):
        go(rcopy(part.at[a, :, 1 - c], sib.at[a], rs1.at[a], rr1.at[a], sq=q_sib))

    def sum_far(a):
        rcopy(part.at[a, :, 1 - c], sib.at[a], rs1.at[a], rr1.at[a], sq=q_sib).wait_recv()
        red[a, x_far] = part[a, x_far, c] + sib[a, x_far]
        up, low = red.at[a, x_far, half_up], red.at[a, x_far, half_low]
        go(rcopy(up, half.at[a, 0], rs2.at[a, 0], rr2.at[a, 0], sq=q_right))
        go(rcopy(low, half.at[a, 1], rs2.at[a, 1], rr2.at[a, 1], sq=q_left))
        red[a, x_right] = part[a, x_right, c] + sib[a, x_right]
        red[a, x_left] = part[a, x_left, c] + sib[a, x_left]
        red[a, x] = part[a, x, c] + sib[a, x]

    def sum_near(a):
        rcopy(half.at[a, 0], half.at[a, 0], rs2.at[a, 0], rr2.at[a, 0], sq=q_right).wait_recv()
        red[a, x_right, half_up] = red[a, x_right, half_up] + half[a, 0]
        go(rcopy(red.at[a, x_right], full.at[a, 0], rs2.at[a, 2], rr2.at[a, 2], sq=q_right))
        rcopy(half.at[a, 1], half.at[a, 1], rs2.at[a, 1], rr2.at[a, 1], sq=q_left).wait_recv()
        red[a, x_left, half_low] = red[a, x_left, half_low] + half[a, 1]
        go(rcopy(red.at[a, x_left], full.at[a, 1], rs2.at[a, 3], rr2.at[a, 3], sq=q_left))

    def sum_end(a):
        rcopy(full.at[a, 0], full.at[a, 0], rs2.at[a, 2], rr2.at[a, 2], sq=q_right).wait_recv()
        rcopy(full.at[a, 1], full.at[a, 1], rs2.at[a, 3], rr2.at[a, 3], sq=q_left).wait_recv()
        outs[a][...] = red[a, x] + (full[a, 0] + full[a, 1])

    for k in range(3):
        blk = att.at[lax.rem(s + 3 - k, 4)]
        rcopy(blk, blk, ts.at[k], tr.at[k], sg=seg_at(k)).wait_recv()
    asp = split(att[...].reshape(512, 256))
    dw = dot3((oghi[...].reshape(512, 1024), oglo[...].reshape(512, 1024)), asp, TN)
    put(2, dw, pl.ds(0, 256))
    sum_start(2)

    for k in range(3):
        rcopy(psend.at[k], dpart.at[k], ds.at[k], dr.at[k], sg=seg_at(k)).wait_recv()
    datt = (psend[3] + dpart[0]) + (dpart[1] + dpart[2])
    dsp = [split(datt[:, h * HD:(h + 1) * HD]) for h in range(2)]
    for h in range(2):
        put(1, dot3((phi[h], plo[h]), dsp[h], NN), pl.ds(h * HD, HD))
    sum_start(1)
    sum_far(2)
    ssp = []
    for h in range(2):
        cols = pl.ds(h * HD, HD)
        dp = dot3((vhi[:, cols], vlo[:, cols]), dsp[h], NT)
        p = pt[h]
        dsc = p * (dp - jnp.sum(p * dp, axis=0, keepdims=True))
        phi[h], plo[h] = split(dsc)
        put(0, dot3((phi[h], plo[h]), qsp[h], NN), cols)
    sum_start(0)
    sum_near(2)
    sum_far(1)
    sum_far(0)
    sum_near(1)
    sum_near(0)
    for h in range(2):
        cols = pl.ds(h * HD, HD)
        dq = dot3((phi[h], plo[h]), (khi[:, cols], klo[:, cols]), TN)
        dq_ref[:, cols] = dq * (1.0 / math.sqrt(HD))
    sum_end(2)
    sum_end(1)
    sum_end(0)

    for cp in sends:
        cp.wait_send()
    for mine, cp in ysend:
        @pl.when(jnp.logical_not(mine))
        def _():
            cp.wait_send()

    @pl.when(odd == 0)
    def _():
        for k in range(4):
            zcopy(0, k, zo.at[k, 0], 1).wait_send()
            zcopy(0, k, zo.at[k, 1], -1).wait_send()

    @pl.when(odd == 1)
    def _():
        for k in range(4):
            zcopy(3, k, zs.at[k, 2], 1).wait_send()


def shards(query, key_in, value, out_grad, w_out):
    blk = (128, 256)
    vmem = pl.BlockSpec(memory_space=pltpu.VMEM)
    sem = lambda *n: pltpu.SemaphoreType.DMA(n)
    outs = pl.pallas_call(
        body,
        out_shape=[jax.ShapeDtypeStruct(blk, F32)] * 4,
        in_specs=[vmem] * 5,
        out_specs=[vmem] * 4,
        scratch_shapes=[
            pltpu.VMEM((3, 8, 128, 256), F32),
            pltpu.VMEM((4, 4, 2, 128, 128), F32),
            pltpu.VMEM((4, 128, 1024), BF16),
            pltpu.VMEM((4, 128, 1024), BF16),
            pltpu.VMEM((4, 128, 256), F32),
            pltpu.VMEM((4, 128, 256), F32),
            pltpu.VMEM((3, 128, 256), F32),
            pltpu.VMEM((3, 4, 2, 128, 256), F32),
            pltpu.VMEM((3, 4, 128, 256), F32),
            pltpu.VMEM((3, 4, 128, 256), F32),
            pltpu.VMEM((3, 2, 64, 256), F32),
            pltpu.VMEM((3, 2, 128, 256), F32),
        ]
        + [pltpu.VMEM((1024, 256), BF16)] * 6
        + [
            pltpu.VMEM((2, 1024, 128), F32),
            pltpu.VMEM((2, 1024, 128), BF16),
            pltpu.VMEM((2, 1024, 128), BF16),
            sem(3, 4), sem(3, 4), sem(3, 4), sem(3, 4),
            sem(2, 2), sem(4, 2),
            sem(4, 3), sem(4, 2), sem(4, 4),
            sem(3), sem(3), sem(3), sem(3),
            sem(3), sem(3), sem(3, 4), sem(3, 4),
        ],
        compiler_params=pltpu.CompilerParams(
            collective_id=0, has_side_effects=True, vmem_limit_bytes=48 * 1024 * 1024
        ),
        cost_estimate=pl.CostEstimate(
            flops=3 * 940_000_000, bytes_accessed=1_200_000, transcendentals=262_144
        ),
    )(query[0], key_in[0], value[0], out_grad[0], w_out)
    dq, dk, dv, dw = outs
    return dq[None], dk[None], dv[None], dw


def solution(mesh):
    act = P("sg", "sq", "tp")
    wsp = P(("sq", "sg"), "tp")
    return jax.shard_map(
        shards,
        mesh=mesh,
        in_specs=(act, act, act, act, wsp),
        out_specs=(act, act, act, wsp),
        check_vma=False,
    )
```

```python
import math

import jax
import jax.numpy as jnp
from jax import lax
from jax.experimental import pallas as pl
from jax.experimental.pallas import tpu as pltpu
from jax.sharding import PartitionSpec as P

HD = 128
F32 = jnp.float32
BF16 = jnp.bfloat16
NN = (((1,), (0,)), ((), ()))
NT = (((1,), (1,)), ((), ()))
TN = (((0,), (0,)), ((), ()))


def rcopy(src, dst, ssem, rsem, **dev):
    return pltpu.make_async_remote_copy(
        src_ref=src,
        dst_ref=dst,
        send_sem=ssem,
        recv_sem=rsem,
        device_id=dev,
        device_id_type=pl.DeviceIdType.MESH,
    )


def split(x):
    hi = x.astype(BF16)
    return hi, (x - hi.astype(F32)).astype(BF16)


def dot3(a, b, dims):
    d = lambda u, v: lax.dot_general(u, v, dims, preferred_element_type=F32)
    return d(a[0], b[0]) + (d(a[0], b[1]) + d(a[1], b[0]))


def body(
    q_ref, k_ref, v_ref, og_ref, w_ref,
    dq_ref, dk_ref, dv_ref, dw_ref,
    qh, kv, wb, ogb, oghi, oglo, att, ahi, alo, psend, dpart, dqs,
    wpart, wsib, wred, whalf, wfull, part, half, near_in, own_in,
    qhi, qlo, khi, klo, vhi, vlo, whi, wlo, pt, phi, plo,
    lin, qs_s, qs_r, kxs, kxr, kss, ksr, xs, xr, ss, sr, ys, yr, zs, zo, zr,
    ts, tr, ds, dr, ws1, wr1, ws2, wr2, hs, hr, fs, fr, os, orr, qos, qor,
):
    t = lax.axis_index("tp")
    q = lax.axis_index("sq")
    s = lax.axis_index("sg")
    yh, z = lax.div(t, 8), lax.rem(t, 8)
    x, c = lax.div(q, 2), lax.rem(q, 2)
    par = lax.div(s, 2)
    odd = lax.rem(z + par, 2)
    ring = lambda d: yh * 8 + lax.rem(z + d + 8, 8)
    x_right, x_left, x_far = lax.rem(x + 1, 4), lax.rem(x + 3, 4), lax.rem(x + 2, 4)
    q_right, q_left, q_far, q_sib = x_right * 2 + c, x_left * 2 + c, x_far * 2 + c, x * 2 + 1 - c
    sibling = lambda b: b + 1 - 2 * c
    seg_at = lambda k: lax.rem(s + 1 + k, 4)
    half_cols = lambda i: pl.ds(pl.multiple_of(i * HD, HD), HD)
    up, low = pl.ds(0, 64), pl.ds(64, 64)

    barrier = pltpu.get_barrier_semaphore()
    partners = []
    for d in range(4):
        partners.append({"tp": (1 - yh) * 8 + z, "sg": lax.rem(s + d, 4)})
        for core in range(2):
            if d > 0:
                partners.append({"sg": lax.rem(s + d, 4), "sq": x * 2 + core})
                if d != 2:
                    partners.append({"sq": lax.rem(x + d, 4) * 2 + core})
    partners += [{"tp": ring(1)}, {"tp": ring(-1)}, {"sq": q_sib}]
    for p in partners:
        pl.semaphore_signal(barrier, inc=1, device_id=p, device_id_type=pl.DeviceIdType.MESH)
    pl.semaphore_wait(barrier, len(partners))

    sends = []

    def go(copy):
        copy.start()
        sends.append(copy)

    zi_own = lax.div(z, 2)
    ysend = []
    for h in range(2):
        target = 2 * lax.rem(z, 2) + h
        nearer = jnp.where(jnp.abs(s - target) == 3, 1 - yh, yh)
        for i, y in enumerate((nearer, 1 - nearer)):
            mine = jnp.logical_and(yh == y, s == target)
            cp = rcopy(
                og_ref.at[:, pl.ds(h * HD, HD)],
                ogb.at[zi_own, s, yh],
                ys.at[h, i],
                yr.at[s, yh],
                tp=y * 8 + z,
                sg=target,
            )
            ysend.append((jnp.logical_not(mine), cp))
    for i in (0, 2):
        pl.when(ysend[i][0])(ysend[i][1].start)

    og_mine = og_ref.at[:, half_cols(lax.rem(s, 2))]
    og_local = pltpu.make_async_copy(og_mine, ogb.at[zi_own, s, yh], lin.at[4])

    nearer = [jnp.where(jnp.abs(seg_at(k) - s) == 3, 1 - yh, yh) for k in range(3)]
    pieces = [(s, yh)]
    pieces += [(seg_at(k), nearer[k]) for k in range(3)]
    pieces += [(seg_at(k), 1 - nearer[k]) for k in range(3)]
    pieces.append((s, 1 - yh))

    def zcopy(d, n, sem, step):
        zi = lax.div(lax.rem(z - d + 16, 8), 2)
        j, y = pieces[n]
        ref = ogb.at[zi, j, y]
        src = og_mine if d == 0 and n == 0 else ref
        return rcopy(src, ref, sem, zr.at[n, zi], tp=ring(step))

    def own(n):
        if n > 0:
            j, y = pieces[n]
            blk = ogb.at[zi_own, j, y]
            rcopy(blk, blk, ys.at[0, 0], yr.at[j, y], tp=t, sg=s).wait_recv()
        zcopy(0, n, zo.at[n, 0], 1).start()
        zcopy(0, n, zo.at[n, 1], -1).start()

    @pl.when(odd == 0)
    def _():
        own(0)
        og_local.start()

    kv_in = (k_ref, v_ref)
    for a in range(2):
        for side, xo in enumerate((x_right, x_left)):
            for core in range(2):
                go(rcopy(kv_in[a].at[:, pl.ds(core * HD, HD)], kv.at[a, q],
                         kxs.at[a, side, core], kxr.at[a, side, c], sq=xo * 2 + core))
        go(rcopy(kv_in[a].at[:, half_cols(1 - c)], kv.at[a, q], kss.at[a], ksr.at[a], sq=q_sib))
    go(rcopy(q_ref.at[:, half_cols(1 - c)], qh.at[c], qs_s, qs_r, sq=q_sib))
    go(rcopy(w_ref, wb.at[q], xs.at[0], xr.at[0], sq=q_right))
    go(rcopy(w_ref, wb.at[q], xs.at[1], xr.at[1], sq=q_left))
    go(rcopy(w_ref, wb.at[q], ss.at[0], sr.at[0], sq=q_sib))
    local = [pltpu.make_async_copy(kv_in[a].at[:, half_cols(c)], kv.at[a, q], lin.at[a]) for a in range(2)]
    local.append(pltpu.make_async_copy(w_ref, wb.at[q], lin.at[2]))
    local.append(pltpu.make_async_copy(q_ref.at[:, half_cols(c)], qh.at[c], lin.at[3]))
    for cp in local:
        cp.start()
    for i in (0, 2):
        pl.when(ysend[i][0])(ysend[i][1].wait_send)
        ysend[i + 1][1].start()

    def kv_copy(a, side, core, xs_, xd, rows=None, hop=0):
        blk = kv.at[a, xs_ * 2 + core]
        if rows is not None:
            blk = kv.at[a, xs_ * 2 + core, rows]
        return rcopy(blk, blk, kxs.at[a, side + 2 * hop, core], kxr.at[a, side + 2 * hop, core], sq=xd * 2 + c)

    def kv_near(a):
        for side, (xs_, xd, rows) in enumerate(((x_left, x_right, up), (x_right, x_left, low))):
            for core in range(2):
                kv_copy(a, side, core, xs_, xd).wait_recv()
                go(kv_copy(a, side, core, xs_, xd, rows, 1))

    def kv_done(a):
        for core in range(2):
            kv_copy(a, 0, core, x_far, x_right, up, 1).wait_recv()
            kv_copy(a, 1, core, x_far, x_left, low, 1).wait_recv()
        rcopy(kv.at[a, q_sib], kv.at[a, q_sib], kss.at[a], ksr.at[a], sq=q_sib).wait_recv()
        local[a].wait()

    def w_near():
        blk = wb.at[q_left]
        rcopy(blk, blk, xs.at[0], xr.at[0], sq=q_right).wait_recv()
        hb = wb.at[q_left, up]
        go(rcopy(hb, hb, xs.at[2], xr.at[2], sq=q_right))
        go(rcopy(blk, blk, ss.at[1], sr.at[1], sq=q_sib))
        blk = wb.at[q_right]
        rcopy(blk, blk, xs.at[1], xr.at[1], sq=q_left).wait_recv()
        hb = wb.at[q_right, low]
        go(rcopy(hb, hb, xs.at[3], xr.at[3], sq=q_left))
        go(rcopy(blk, blk, ss.at[2], sr.at[2], sq=q_sib))

    def w_far():
        for i, rows in enumerate((up, low)):
            hb = wb.at[q_far, rows]
            rcopy(hb, hb, xs.at[2 + i], xr.at[2 + i], sq=q_right).wait_recv()
        blk = wb.at[q_far]
        go(rcopy(blk, blk, ss.at[3], sr.at[3], sq=q_sib))

    def w_done():
        for i, b in enumerate((q, q_left, q_right, q_far)):
            blk = wb.at[sibling(b)]
            rcopy(blk, blk, ss.at[i], sr.at[i], sq=q_sib).wait_recv()
        local[2].wait()
        for b in range(8):
            rows = pl.ds(b * 128, 128)
            whi[rows, :], wlo[rows, :] = split(wb[b])

    def pass_near(n, odd):
        cp = zcopy(2 - odd, n, zs.at[n, 0], 1)
        cp.wait_recv()
        cp.start()
        cp = zcopy(6 + odd, n, zs.at[n, 1], -1)
        cp.wait_recv()
        cp.start()

    def pass_far(n):
        cp = zcopy(3, n, zs.at[n, 2], 1) if n % 2 == 0 else zcopy(5, n, zs.at[n, 2], -1)
        cp.wait_recv()
        cp.start()

    def ring_steps(owns=(), near_even=(), near_odd=(), fars=()):
        @pl.when(odd == 0)
        def _():
            for n in owns:
                own(n)
            for n in near_even:
                pass_near(n, 0)

        @pl.when(odd == 1)
        def _():
            for n in near_odd:
                pass_near(n, 1)
            for n in fars:
                pass_far(n)

    def arrived(n):
        @pl.when(odd == 0)
        def _():
            zcopy(4, n, zs.at[n, 2], 1).wait_recv()

        @pl.when(odd == 1)
        def _():
            zcopy(5 if n % 2 == 0 else 3, n, zs.at[n, 2], 1).wait_recv()

    def partial_dot(k):
        j = seg_at(k)
        for zi in range(4):
            for y in range(2):
                hi, lo = split(ogb[zi, j, y])
                cols = pl.ds((y * 4 + zi) * HD, HD)
                oghi[j, :, cols] = hi
                oglo[j, :, cols] = lo
        res = dot3((oghi[j], oglo[j]), (whi[...], wlo[...]), NN)
        psend[k, 0] = res[:, :HD]
        psend[k, 1] = res[:, HD:]
        if k < 3:
            for core in range(2):
                go(rcopy(psend.at[k, core], dpart.at[k, c], ds.at[k, core], dr.at[k, c], sg=j, sq=x * 2 + core))
        else:
            go(rcopy(psend.at[3, 1 - c], dpart.at[3, c], ds.at[3, 0], dr.at[3, c], sq=q_sib))
            dpart[3, c] = psend[3, c]

    def probs():
        rcopy(qh.at[1 - c], qh.at[1 - c], qs_s, qs_r, sq=q_sib).wait_recv()
        local[3].wait()
        qhi[...], qlo[...] = split(qh[...].reshape(256, HD) * (1.0 / math.sqrt(HD)))
        kv_done(0)
        khi[...], klo[...] = split(kv[0].reshape(1024, HD))
        st = dot3((khi[...], klo[...]), (qhi[...], qlo[...]), NT)
        e = jnp.exp(st - jnp.max(st, axis=0, keepdims=True))
        p = e / jnp.sum(e, axis=0, keepdims=True)
        pt[...] = p
        phi[...], plo[...] = split(p)

    tsends = []

    def to(copy):
        copy.start()
        tsends.append(copy)

    def attend():
        kv_done(1)
        vhi[...], vlo[...] = split(kv[1].reshape(1024, HD))
        res = dot3((phi[...], plo[...]), (vhi[...], vlo[...]), TN)
        dqs[...] = res.reshape(2, 128, HD)
        for k in range(3):
            for core in range(2):
                to(rcopy(dqs.at[core], att.at[s, c], ts.at[k, core], tr.at[k, c], sg=seg_at(k), sq=x * 2 + core))
        to(rcopy(dqs.at[1 - c], att.at[s, c], ts.at[3, 0], tr.at[3, c], sq=q_sib))
        att[s, c] = dqs[c]

    ring_steps(owns=(1,), near_odd=(0,))
    kv_near(0)
    ring_steps(owns=(2, 3), near_odd=(1,))
    kv_near(1)
    ring_steps(owns=(4,), near_even=(0,), near_odd=(2,))
    w_near()
    ring_steps(owns=(5, 6, 7), near_odd=(3,))
    probs()
    ring_steps(near_even=(1,), near_odd=(4,), fars=(0,))
    attend()
    ring_steps(near_even=(2,), near_odd=(5,), fars=(1,))
    w_far()
    ring_steps(near_even=(3,), near_odd=(6,))
    w_done()
    ring_steps(near_odd=(7,))
    ring_steps(near_even=(4,), fars=(2,))
    ring_steps(near_even=(5,), fars=(3,))
    ring_steps(near_even=(6,), fars=(4,))
    arrived(1)
    arrived(4)
    partial_dot(0)
    ring_steps(near_even=(7,), fars=(5,))
    arrived(2)
    arrived(5)
    partial_dot(1)
    ring_steps(fars=(6,))
    ring_steps(fars=(7,))
    arrived(3)
    arrived(6)
    partial_dot(2)

    @pl.when(odd == 0)
    def _():
        og_local.wait()

    arrived(0)
    arrived(7)
    partial_dot(3)

    for k in range(3):
        for head in range(2):
            blk = att.at[lax.rem(s + 3 - k, 4), head]
            rcopy(blk, blk, ts.at[k, 0], tr.at[k, head], sq=q_sib).wait_recv()
    blk = att.at[s, 1 - c]
    rcopy(blk, blk, ts.at[3, 0], tr.at[3, 1 - c], sq=q_sib).wait_recv()
    for head in range(2):
        cols = pl.ds(head * HD, HD)
        ahi[:, cols], alo[:, cols] = split(att[:, head].reshape(512, HD))
    dw = dot3(
        (oghi[...].reshape(512, 1024), oglo[...].reshape(512, 1024)), (ahi[...], alo[...]), TN
    )
    wpart[...] = dw.reshape(4, 2, 128, 256)
    go(rcopy(wpart.at[:, 1 - c], wsib, ws1, wr1, sq=q_sib))

    def dw_far():
        rcopy(wpart.at[:, 1 - c], wsib, ws1, wr1, sq=q_sib).wait_recv()
        wred[x_far] = wpart[x_far, c] + wsib[x_far]
        go(rcopy(wred.at[x_far, up], whalf.at[0], ws2.at[0], wr2.at[0], sq=q_right))
        go(rcopy(wred.at[x_far, low], whalf.at[1], ws2.at[1], wr2.at[1], sq=q_left))
        wred[x_right] = wpart[x_right, c] + wsib[x_right]
        go(rcopy(wred.at[x_right, low], wfull.at[0, low], ws2.at[2], wr2.at[2], sq=q_right))
        wred[x_left] = wpart[x_left, c] + wsib[x_left]
        go(rcopy(wred.at[x_left, up], wfull.at[1, up], ws2.at[3], wr2.at[3], sq=q_left))
        wred[x] = wpart[x, c] + wsib[x]

    def dw_near():
        rcopy(whalf.at[0], whalf.at[0], ws2.at[0], wr2.at[0], sq=q_right).wait_recv()
        wred[x_right, up] = wred[x_right, up] + whalf[0]
        go(rcopy(wred.at[x_right, up], wfull.at[0, up], ws2.at[4], wr2.at[4], sq=q_right))
        rcopy(whalf.at[1], whalf.at[1], ws2.at[1], wr2.at[1], sq=q_left).wait_recv()
        wred[x_left, low] = wred[x_left, low] + whalf[1]
        go(rcopy(wred.at[x_left, low], wfull.at[1, low], ws2.at[5], wr2.at[5], sq=q_left))

    def dw_end():
        for i, (side, rows) in enumerate(((0, low), (1, up), (0, up), (1, low))):
            blk = wfull.at[side, rows]
            rcopy(blk, blk, ws2.at[2 + i], wr2.at[2 + i], sq=q_right).wait_recv()
        dw_ref[...] = wred[x] + (wfull[0] + wfull[1])

    def near_rows(a, side, stage, xd, rows):
        for core in range(2):
            go(rcopy(part.at[a, xd, core, rows], near_in.at[a, side, c, rows],
                     fs.at[a, side, stage, core], fr.at[a, side, stage, c], sq=xd * 2 + core))

    def sum_start(a, val):
        part[a] = val.reshape(4, 2, 128, HD)
        go(rcopy(part.at[a, x_far, :, up], half.at[a, 0], hs.at[a, 0], hr.at[a, 0], sq=q_right))
        go(rcopy(part.at[a, x_far, :, low], half.at[a, 1], hs.at[a, 1], hr.at[a, 1], sq=q_left))
        near_rows(a, 0, 0, x_right, low)
        near_rows(a, 1, 0, x_left, up)
        go(rcopy(part.at[a, x, 1 - c], own_in.at[a], os.at[a], orr.at[a], sq=q_sib))

    def sum_near(a):
        rcopy(half.at[a, 0], half.at[a, 0], hs.at[a, 0], hr.at[a, 0], sq=q_right).wait_recv()
        part[a, x_right, :, up] = part[a, x_right, :, up] + half[a, 0]
        near_rows(a, 0, 1, x_right, up)
        rcopy(half.at[a, 1], half.at[a, 1], hs.at[a, 1], hr.at[a, 1], sq=q_left).wait_recv()
        part[a, x_left, :, low] = part[a, x_left, :, low] + half[a, 1]
        near_rows(a, 1, 1, x_left, low)

    outs = (dk_ref, dv_ref)

    def sum_end(a):
        for side in range(2):
            for stage in range(2):
                rows = low if side == stage else up
                for core in range(2):
                    blk = near_in.at[a, side, core, rows]
                    rcopy(blk, blk, fs.at[a, side, stage, core], fr.at[a, side, stage, core], sq=q_right).wait_recv()
        rcopy(own_in.at[a], own_in.at[a], os.at[a], orr.at[a], sq=q_sib).wait_recv()
        outs[a][:, half_cols(c)] = part[a, x, c] + (near_in[a, 0, c] + near_in[a, 1, c])
        outs[a][:, half_cols(1 - c)] = own_in[a] + (near_in[a, 0, 1 - c] + near_in[a, 1, 1 - c])

    dw_far()
    for k in range(3):
        for core in range(2):
            blk = dpart.at[k, core]
            rcopy(blk, blk, ds.at[k, 0], dr.at[k, core], sq=q_sib).wait_recv()
    blk = dpart.at[3, 1 - c]
    rcopy(blk, blk, ds.at[3, 0], dr.at[3, 1 - c], sq=q_sib).wait_recv()
    datt = ((dpart[0] + dpart[1]) + (dpart[2] + dpart[3])).reshape(256, HD)
    dsp = split(datt)
    sum_start(1, dot3((phi[...], plo[...]), dsp, NN))
    dp = dot3((vhi[...], vlo[...]), dsp, NT)
    p = pt[...]
    dsc = p * (dp - jnp.sum(p * dp, axis=0, keepdims=True))
    phi[...], plo[...] = split(dsc)
    sum_start(0, dot3((phi[...], plo[...]), (qhi[...], qlo[...]), NN))
    dw_near()
    sum_near(1)
    sum_near(0)
    for cp in tsends:
        cp.wait_send()
    dq = dot3((phi[...], plo[...]), (khi[...], klo[...]), TN) * (1.0 / math.sqrt(HD))
    dqs[...] = dq.reshape(2, 128, HD)
    go(rcopy(dqs.at[1 - c], dq_ref.at[:, half_cols(c)], qos, qor, sq=q_sib))
    dq_ref[:, half_cols(c)] = dqs[c]
    dw_end()
    sum_end(1)
    sum_end(0)
    rcopy(dqs.at[1 - c], dq_ref.at[:, half_cols(1 - c)], qos, qor, sq=q_sib).wait_recv()

    for cp in sends:
        cp.wait_send()
    for i in (1, 3):
        ysend[i][1].wait_send()

    @pl.when(odd == 0)
    def _():
        for n in range(8):
            zcopy(0, n, zo.at[n, 0], 1).wait_send()
            zcopy(0, n, zo.at[n, 1], -1).wait_send()

    @pl.when(odd == 1)
    def _():
        for n in range(8):
            zcopy(3, n, zs.at[n, 2], 1).wait_send()

    for n in range(8):
        for i in range(2):
            zcopy(3, n, zs.at[n, i], 1).wait_send()


def shards(query, key_in, value, out_grad, w_out):
    blk = (128, 256)
    vmem = pl.BlockSpec(memory_space=pltpu.VMEM)
    hbm = pl.BlockSpec(memory_space=pl.ANY)
    sem = lambda *n: pltpu.SemaphoreType.DMA(n)
    one = pltpu.SemaphoreType.DMA
    f32 = lambda *n: pltpu.VMEM(n, F32)
    b16 = lambda *n: pltpu.VMEM(n, BF16)
    outs = pl.pallas_call(
        body,
        out_shape=[jax.ShapeDtypeStruct(blk, F32)] * 4,
        in_specs=[hbm] * 5,
        out_specs=[vmem] * 4,
        scratch_shapes=[
            f32(2, 128, 128),
            f32(2, 8, 128, 128),
            f32(8, 128, 256),
            f32(4, 4, 2, 128, 128),
            b16(4, 128, 1024), b16(4, 128, 1024),
            f32(4, 2, 128, 128),
            b16(512, 256), b16(512, 256),
            f32(4, 2, 128, 128),
            f32(4, 2, 128, 128),
            f32(2, 128, 128),
            f32(4, 2, 128, 256),
            f32(4, 128, 256),
            f32(4, 128, 256),
            f32(2, 64, 256),
            f32(2, 128, 256),
            f32(2, 4, 2, 128, 128),
            f32(2, 2, 2, 64, 128),
            f32(2, 2, 2, 128, 128),
            f32(2, 128, 128),
            b16(256, 128), b16(256, 128),
            b16(1024, 128), b16(1024, 128),
            b16(1024, 128), b16(1024, 128),
            b16(1024, 256), b16(1024, 256),
            f32(1024, 256),
            b16(1024, 256), b16(1024, 256),
            sem(5), one, one,
            sem(2, 4, 2), sem(2, 4, 2), sem(2), sem(2),
            sem(4), sem(4), sem(4), sem(4),
            sem(2, 2), sem(4, 2),
            sem(8, 3), sem(8, 2), sem(8, 4),
            sem(4, 2), sem(4, 2), sem(4, 2), sem(4, 2),
            one, one, sem(6), sem(6),
            sem(2, 2), sem(2, 2),
            sem(2, 2, 2, 2), sem(2, 2, 2, 2),
            sem(2), sem(2), one, one,
        ],
        compiler_params=pltpu.CompilerParams(
            collective_id=0, has_side_effects=True, vmem_limit_bytes=60 * 1024 * 1024
        ),
        cost_estimate=pl.CostEstimate(
            flops=3 * 940_000_000, bytes_accessed=1_200_000, transcendentals=262_144
        ),
    )(query[0], key_in[0], value[0], out_grad[0], w_out)
    dq, dk, dv, dw = outs
    return dq[None], dk[None], dv[None], dw


def solution(mesh):
    act = P("sg", "sq", "tp")
    wsp = P(("sq", "sg"), "tp")
    return jax.shard_map(
        shards,
        mesh=mesh,
        in_specs=(act, act, act, act, wsp),
        out_specs=(act, act, act, wsp),
        check_vma=False,
    )
```

```python
import math

import jax
import jax.numpy as jnp
from jax import lax
from jax.experimental import pallas as pl
from jax.experimental.pallas import tpu as pltpu
from jax.sharding import PartitionSpec as P

HD = 128
F32 = jnp.float32
BF16 = jnp.bfloat16
NN = (((1,), (0,)), ((), ()))
NT = (((1,), (1,)), ((), ()))
TN = (((0,), (0,)), ((), ()))


def rcopy(src, dst, ssem, rsem, **dev):
    return pltpu.make_async_remote_copy(
        src_ref=src,
        dst_ref=dst,
        send_sem=ssem,
        recv_sem=rsem,
        device_id=dev,
        device_id_type=pl.DeviceIdType.MESH,
    )


def split(x):
    hi = x.astype(BF16)
    return hi, (x - hi.astype(F32)).astype(BF16)


def dot3(a, b, dims):
    d = lambda u, v: lax.dot_general(u, v, dims, preferred_element_type=F32)
    return d(a[0], b[0]) + (d(a[0], b[1]) + d(a[1], b[0]))


def body(
    q_ref, k_ref, v_ref, og_ref, w_ref,
    dq_ref, dk_ref, dv_ref, dw_ref,
    qh, kv, wb, ogb, oghi, oglo, att, ahi, alo, psend, dpart, dqs,
    wpart, wsib, wred, whalf, wfull, part, half, near_in, own_in,
    qhi, qlo, khi, klo, vhi, vlo, whi, wlo, pt, phi, plo,
    lin, qs_s, qs_r, kxs, kxr, kss, ksr, xs, xr, ss, sr, ys, yr, zs, zo, zr,
    ts, tr, tf_s, tf_r, ds, dr, ws1, wr1, ws2, wr2, hs, hr, fs, fr, os, orr, qos, qor,
):
    t = lax.axis_index("tp")
    q = lax.axis_index("sq")
    s = lax.axis_index("sg")
    yh, z = lax.div(t, 8), lax.rem(t, 8)
    x, c = lax.div(q, 2), lax.rem(q, 2)
    par = lax.div(s, 2)
    odd = lax.rem(z + par, 2)
    ring = lambda d: yh * 8 + lax.rem(z + d + 8, 8)
    x_right, x_left, x_far = lax.rem(x + 1, 4), lax.rem(x + 3, 4), lax.rem(x + 2, 4)
    q_right, q_left, q_far, q_sib = x_right * 2 + c, x_left * 2 + c, x_far * 2 + c, x * 2 + 1 - c
    sibling = lambda b: b + 1 - 2 * c
    seg_at = lambda k: lax.rem(s + (2, 1, 3, 4)[k], 4)
    half_cols = lambda i: pl.ds(pl.multiple_of(i * HD, HD), HD)
    up, low = pl.ds(0, 64), pl.ds(64, 64)
    wup, wlow = pl.ds(0, 128), pl.ds(128, 128)

    barrier = pltpu.get_barrier_semaphore()
    partners = []
    for d in range(4):
        partners.append({"tp": (1 - yh) * 8 + z, "sg": lax.rem(s + d, 4)})
        for core in range(2):
            if d > 0:
                partners.append({"sg": lax.rem(s + d, 4), "sq": x * 2 + core})
                if d != 2:
                    partners.append({"sq": lax.rem(x + d, 4) * 2 + core})
    partners += [{"tp": ring(1)}, {"tp": ring(-1)}, {"sq": q_sib}]
    for p in partners:
        pl.semaphore_signal(barrier, inc=1, device_id=p, device_id_type=pl.DeviceIdType.MESH)
    pl.semaphore_wait(barrier, len(partners))

    sends = []

    def go(copy):
        copy.start()
        sends.append(copy)

    zi_own = lax.div(z, 2)
    ysend = []
    first = jnp.where(lax.rem(s - 2 * lax.rem(z, 2) + 7, 4) < 2, 0, 1)
    for i, h in enumerate((first, 1 - first)):
        target = 2 * lax.rem(z, 2) + h
        nearer = jnp.where(jnp.abs(s - target) == 3, 1 - yh, yh)
        for y in (nearer, 1 - nearer):
            cp = rcopy(
                og_ref.at[:, half_cols(h)],
                ogb.at[zi_own, s, yh],
                ys.at[len(ysend)],
                yr.at[s, yh],
                tp=y * 8 + z,
                sg=target,
            )
            ysend.append(cp)
            if len(ysend) == 3:
                other = jnp.logical_or(yh != y, s != target)
                pl.when(other)(cp.start)
            else:
                cp.start()

    og_mine = og_ref.at[:, half_cols(lax.rem(s, 2))]
    og_local = pltpu.make_async_copy(og_mine, ogb.at[zi_own, s, yh], lin.at[4])

    pieces = [(s, yh)]
    for k in range(3):
        nearer = jnp.where(jnp.abs(seg_at(k) - s) == 3, 1 - yh, yh)
        pieces += [(seg_at(k), nearer), (seg_at(k), 1 - nearer)]
    pieces.append((s, 1 - yh))

    def zcopy(d, n, sem, step):
        zi = lax.div(lax.rem(z - d + 16, 8), 2)
        j, y = pieces[n]
        ref = ogb.at[zi, j, y]
        src = og_mine if d == 0 and n == 0 else ref
        return rcopy(src, ref, sem, zr.at[n, zi], tp=ring(step))

    def own(n):
        if n > 0:
            j, y = pieces[n]
            blk = ogb.at[zi_own, j, y]
            rcopy(blk, blk, ys.at[0], yr.at[j, y], tp=t, sg=s).wait_recv()
        zcopy(0, n, zo.at[n, 0], 1).start()
        zcopy(0, n, zo.at[n, 1], -1).start()

    @pl.when(odd == 0)
    def _():
        own(0)
        og_local.start()

    kv_in = (k_ref, v_ref)
    for a in range(2):
        for side, xo in enumerate((x_right, x_left)):
            for core in range(2):
                go(rcopy(kv_in[a].at[:, pl.ds(core * HD, HD)], kv.at[a, q],
                         kxs.at[a, side, core], kxr.at[a, side, c], sq=xo * 2 + core))
        go(rcopy(kv_in[a].at[:, half_cols(1 - c)], kv.at[a, q], kss.at[a], ksr.at[a], sq=q_sib))
    go(rcopy(q_ref.at[:, half_cols(1 - c)], qh.at[c], qs_s, qs_r, sq=q_sib))
    local = [pltpu.make_async_copy(kv_in[a].at[:, half_cols(c)], kv.at[a, q], lin.at[a]) for a in range(2)]
    local.append(pltpu.make_async_copy(w_ref, wb.at[q], lin.at[2]))
    local.append(pltpu.make_async_copy(q_ref.at[:, half_cols(c)], qh.at[c], lin.at[3]))
    for cp in local:
        cp.start()

    def kv_copy(a, side, core, xs_, xd, rows=None, hop=0):
        blk = kv.at[a, xs_ * 2 + core]
        if rows is not None:
            blk = kv.at[a, xs_ * 2 + core, rows]
        return rcopy(blk, blk, kxs.at[a, side + 2 * hop, core], kxr.at[a, side + 2 * hop, core], sq=xd * 2 + c)

    def kv_near(a):
        for side, (xs_, xd, rows) in enumerate(((x_left, x_right, up), (x_right, x_left, low))):
            for core in range(2):
                kv_copy(a, side, core, xs_, xd).wait_recv()
                go(kv_copy(a, side, core, xs_, xd, rows, 1))

    def kv_done(a):
        for core in range(2):
            kv_copy(a, 0, core, x_far, x_right, up, 1).wait_recv()
            kv_copy(a, 1, core, x_far, x_left, low, 1).wait_recv()
        rcopy(kv.at[a, q_sib], kv.at[a, q_sib], kss.at[a], ksr.at[a], sq=q_sib).wait_recv()
        local[a].wait()

    def w_start():
        go(rcopy(w_ref, wb.at[q], xs.at[0], xr.at[0], sq=q_right))
        go(rcopy(w_ref, wb.at[q], xs.at[1], xr.at[1], sq=q_left))
        go(rcopy(w_ref, wb.at[q], ss.at[0], sr.at[0], sq=q_sib))

    def w_near():
        blk = wb.at[q_left]
        rcopy(blk, blk, xs.at[0], xr.at[0], sq=q_right).wait_recv()
        hb = wb.at[q_left, up]
        go(rcopy(hb, hb, xs.at[2], xr.at[2], sq=q_right))
        go(rcopy(blk, blk, ss.at[1], sr.at[1], sq=q_sib))
        blk = wb.at[q_right]
        rcopy(blk, blk, xs.at[1], xr.at[1], sq=q_left).wait_recv()
        hb = wb.at[q_right, low]
        go(rcopy(hb, hb, xs.at[3], xr.at[3], sq=q_left))
        go(rcopy(blk, blk, ss.at[2], sr.at[2], sq=q_sib))

    def w_far():
        for i, rows in enumerate((up, low)):
            hb = wb.at[q_far, rows]
            rcopy(hb, hb, xs.at[2 + i], xr.at[2 + i], sq=q_right).wait_recv()
        blk = wb.at[q_far]
        go(rcopy(blk, blk, ss.at[3], sr.at[3], sq=q_sib))

    def w_done():
        for i, b in enumerate((q, q_left, q_right, q_far)):
            blk = wb.at[sibling(b)]
            rcopy(blk, blk, ss.at[i], sr.at[i], sq=q_sib).wait_recv()
        local[2].wait()
        for b in range(8):
            rows = pl.ds(b * 128, 128)
            whi[rows, :], wlo[rows, :] = split(wb[b])

    on_right, on_left = (0, 2, 4, 1, 6, 3, 5, 7), (1, 3, 0, 5, 2, 7, 4, 6)

    def pass_near(n, odd):
        right, left = (n, n) if odd else (on_right[n], on_left[n])
        cp = zcopy(2 - odd, right, zs.at[right, 0], 1)
        cp.wait_recv()
        cp.start()
        cp = zcopy(6 + odd, left, zs.at[left, 1], -1)
        cp.wait_recv()
        cp.start()

    def pass_far(n):
        cp = zcopy(3, n, zs.at[n, 2], 1) if n % 2 == 0 else zcopy(5, n, zs.at[n, 2], -1)
        cp.wait_recv()
        cp.start()

    def ring_steps(owns=(), near_even=(), near_odd=(), fars=()):
        @pl.when(odd == 0)
        def _():
            for n in owns:
                own(n)
            for n in near_even:
                pass_near(n, 0)

        @pl.when(odd == 1)
        def _():
            for n in near_odd:
                pass_near(n, 1)
            for n in fars:
                pass_far(n)

    def arrived(n):
        @pl.when(odd == 0)
        def _():
            zcopy(4, n, zs.at[n, 2], 1).wait_recv()

        @pl.when(odd == 1)
        def _():
            zcopy(5 if n % 2 == 0 else 3, n, zs.at[n, 2], 1).wait_recv()

    def partial_dot(k):
        j = seg_at(k)
        for zi in range(4):
            for y in range(2):
                hi, lo = split(ogb[zi, j, y])
                cols = pl.ds((y * 4 + zi) * HD, HD)
                oghi[k, :, cols] = hi
                oglo[k, :, cols] = lo
        res = dot3((oghi[k], oglo[k]), (whi[...], wlo[...]), NN)
        psend[k, 0] = res[:, :HD]
        psend[k, 1] = res[:, HD:]
        if k < 3:
            for core in range(2):
                go(rcopy(psend.at[k, core], dpart.at[k, c], ds.at[k, core], dr.at[k, c], sg=j, sq=x * 2 + core))
        else:
            go(rcopy(psend.at[3, 1 - c], dpart.at[3, c], ds.at[3, 0], dr.at[3, c], sq=q_sib))
            dpart[3, c] = psend[3, c]

    def probs():
        rcopy(qh.at[1 - c], qh.at[1 - c], qs_s, qs_r, sq=q_sib).wait_recv()
        local[3].wait()
        qhi[...], qlo[...] = split(qh[...].reshape(256, HD) * (1.0 / math.sqrt(HD)))
        kv_done(0)
        khi[...], klo[...] = split(kv[0].reshape(1024, HD))
        st = dot3((khi[...], klo[...]), (qhi[...], qlo[...]), NT)
        e = jnp.exp(st - jnp.max(st, axis=0, keepdims=True))
        p = e / jnp.sum(e, axis=0, keepdims=True)
        pt[...] = p
        phi[...], plo[...] = split(p)

    ends = (None, s == 3, s == 0)
    inner = jnp.logical_and(s > 0, s < 3)
    far_seg = jnp.where(s == 2, 0, 3)
    tsends, tnear = [], []

    def att_hop(j, to_seg):
        return rcopy(att.at[j], att.at[j], tf_s, tf_r, sg=to_seg)

    def att_forward():
        @pl.when(inner)
        def _():
            for head in range(2):
                blk = att.at[far_seg, head]
                rcopy(blk, blk, ts.at[0, 0], tr.at[0, head], sq=q_sib).wait_recv()
            att_hop(far_seg, 3 - far_seg).start()

    def to(copy):
        copy.start()
        tsends.append(copy)

    def attend():
        kv_done(1)
        vhi[...], vlo[...] = split(kv[1].reshape(1024, HD))
        res = dot3((phi[...], plo[...]), (vhi[...], vlo[...]), TN)
        dqs[...] = res.reshape(2, 128, HD)
        for k in range(3):
            for core in range(2):
                cp = rcopy(dqs.at[core], att.at[s, c], ts.at[k, core], tr.at[k, c], sg=seg_at(k), sq=x * 2 + core)
                if k == 0:
                    to(cp)
                else:
                    pl.when(jnp.logical_not(ends[k]))(cp.start)
                    tnear.append((k, cp))
        to(rcopy(dqs.at[1 - c], att.at[s, c], ts.at[3, 0], tr.at[3, c], sq=q_sib))
        att[s, c] = dqs[c]

    def att_pairs(k):
        j = seg_at(k)
        if k < 3:
            k_from = (0, 2, 1)[k]

            def direct():
                for head in range(2):
                    blk = att.at[j, head]
                    rcopy(blk, blk, ts.at[k_from, 0], tr.at[k_from, head], sq=q_sib).wait_recv()

            if k == 0:
                pl.when(jnp.logical_not(inner))(direct)
            else:
                pl.when(jnp.logical_not(ends[k]))(direct)
                pl.when(ends[k])(att_hop(j, s).wait_recv)
        else:
            blk = att.at[s, 1 - c]
            rcopy(blk, blk, ts.at[3, 0], tr.at[3, 1 - c], sq=q_sib).wait_recv()
        for head in range(2):
            cols = pl.ds(head * HD, HD)
            ahi[k, :, cols], alo[k, :, cols] = split(att[j, head])

    def dw_add(k):
        att_pairs(k)
        att_pairs(k + 1)
        rows = pl.ds(k, 2)
        a = (ahi[rows].reshape(256, 256), alo[rows].reshape(256, 256))
        g = (oghi[rows].reshape(256, 1024), oglo[rows].reshape(256, 1024))
        dw = dot3(a, g, TN)
        for b in range(8):
            part_b = dw[:, b * 128:(b + 1) * 128]
            wpart[b // 2, b % 2] = part_b if k == 0 else wpart[b // 2, b % 2] + part_b

    ring_steps(owns=(1,), near_odd=(0,))
    kv_near(0)
    ring_steps(owns=(2, 3, 4), near_odd=(1,))
    kv_near(1)
    w_start()
    ring_steps(owns=(5, 6), near_odd=(2,))
    probs()
    ring_steps(owns=(7,), near_odd=(3, 4))
    attend()
    ring_steps(near_even=(0,), near_odd=(5,))
    w_near()
    ring_steps(near_even=(1, 2, 3), near_odd=(6, 7))
    w_far()
    ring_steps(near_even=(4,), fars=(0,))
    w_done()
    ring_steps(near_even=(5, 6, 7), fars=(1, 2, 3))
    att_forward()
    ring_steps(fars=(4,))
    arrived(1)
    arrived(2)
    partial_dot(0)
    ring_steps(fars=(5,))
    arrived(3)
    arrived(4)
    partial_dot(1)
    ring_steps(fars=(6, 7))
    arrived(5)
    arrived(6)
    partial_dot(2)
    dw_add(0)

    @pl.when(odd == 0)
    def _():
        og_local.wait()

    arrived(0)
    arrived(7)
    partial_dot(3)
    dw_add(2)
    go(rcopy(wpart.at[:, 1 - c], wsib, ws1, wr1, sq=q_sib))

    def dw_far():
        rcopy(wpart.at[:, 1 - c], wsib, ws1, wr1, sq=q_sib).wait_recv()
        wred[x_far] = wpart[x_far, c] + wsib[x_far]
        go(rcopy(wred.at[x_far, wup], whalf.at[0], ws2.at[0], wr2.at[0], sq=q_right))
        go(rcopy(wred.at[x_far, wlow], whalf.at[1], ws2.at[1], wr2.at[1], sq=q_left))
        wred[x_right] = wpart[x_right, c] + wsib[x_right]
        go(rcopy(wred.at[x_right, wlow], wfull.at[0, wlow], ws2.at[2], wr2.at[2], sq=q_right))
        wred[x_left] = wpart[x_left, c] + wsib[x_left]
        go(rcopy(wred.at[x_left, wup], wfull.at[1, wup], ws2.at[3], wr2.at[3], sq=q_left))
        wred[x] = wpart[x, c] + wsib[x]

    def dw_near():
        rcopy(whalf.at[0], whalf.at[0], ws2.at[0], wr2.at[0], sq=q_right).wait_recv()
        wred[x_right, wup] = wred[x_right, wup] + whalf[0]
        go(rcopy(wred.at[x_right, wup], wfull.at[0, wup], ws2.at[4], wr2.at[4], sq=q_right))
        rcopy(whalf.at[1], whalf.at[1], ws2.at[1], wr2.at[1], sq=q_left).wait_recv()
        wred[x_left, wlow] = wred[x_left, wlow] + whalf[1]
        go(rcopy(wred.at[x_left, wlow], wfull.at[1, wlow], ws2.at[5], wr2.at[5], sq=q_left))

    def dw_end():
        for i, (side, rows) in enumerate(((0, wlow), (1, wup), (0, wup), (1, wlow))):
            blk = wfull.at[side, rows]
            rcopy(blk, blk, ws2.at[2 + i], wr2.at[2 + i], sq=q_right).wait_recv()
        dw_ref[...] = (wred[x] + (wfull[0] + wfull[1])).T

    def near_rows(a, side, stage, xd, rows):
        for core in range(2):
            go(rcopy(part.at[a, xd, core, rows], near_in.at[a, side, c, rows],
                     fs.at[a, side, stage, core], fr.at[a, side, stage, c], sq=xd * 2 + core))

    def sum_start(a, val):
        part[a] = val.reshape(4, 2, 128, HD)
        go(rcopy(part.at[a, x_far, :, up], half.at[a, 0], hs.at[a, 0], hr.at[a, 0], sq=q_right))
        go(rcopy(part.at[a, x_far, :, low], half.at[a, 1], hs.at[a, 1], hr.at[a, 1], sq=q_left))
        near_rows(a, 0, 0, x_right, low)
        near_rows(a, 1, 0, x_left, up)
        go(rcopy(part.at[a, x, 1 - c], own_in.at[a], os.at[a], orr.at[a], sq=q_sib))

    def sum_near(a):
        rcopy(half.at[a, 0], half.at[a, 0], hs.at[a, 0], hr.at[a, 0], sq=q_right).wait_recv()
        part[a, x_right, :, up] = part[a, x_right, :, up] + half[a, 0]
        near_rows(a, 0, 1, x_right, up)
        rcopy(half.at[a, 1], half.at[a, 1], hs.at[a, 1], hr.at[a, 1], sq=q_left).wait_recv()
        part[a, x_left, :, low] = part[a, x_left, :, low] + half[a, 1]
        near_rows(a, 1, 1, x_left, low)

    outs = (dk_ref, dv_ref)

    def sum_end(a):
        for side in range(2):
            for stage in range(2):
                rows = low if side == stage else up
                for core in range(2):
                    blk = near_in.at[a, side, core, rows]
                    rcopy(blk, blk, fs.at[a, side, stage, core], fr.at[a, side, stage, core], sq=q_right).wait_recv()
        rcopy(own_in.at[a], own_in.at[a], os.at[a], orr.at[a], sq=q_sib).wait_recv()
        outs[a][:, half_cols(c)] = part[a, x, c] + (near_in[a, 0, c] + near_in[a, 1, c])
        outs[a][:, half_cols(1 - c)] = own_in[a] + (near_in[a, 0, 1 - c] + near_in[a, 1, 1 - c])

    dw_far()
    for k in range(3):
        for core in range(2):
            blk = dpart.at[k, core]
            rcopy(blk, blk, ds.at[k, 0], dr.at[k, core], sq=q_sib).wait_recv()
    blk = dpart.at[3, 1 - c]
    rcopy(blk, blk, ds.at[3, 0], dr.at[3, 1 - c], sq=q_sib).wait_recv()
    datt = ((dpart[0] + dpart[1]) + (dpart[2] + dpart[3])).reshape(256, HD)
    dsp = split(datt)
    sum_start(1, dot3((phi[...], plo[...]), dsp, NN))
    dp = dot3((vhi[...], vlo[...]), dsp, NT)
    p = pt[...]
    dsc = p * (dp - jnp.sum(p * dp, axis=0, keepdims=True))
    phi[...], plo[...] = split(dsc)
    sum_start(0, dot3((phi[...], plo[...]), (qhi[...], qlo[...]), NN))
    dw_near()
    sum_near(1)
    for cp in tsends:
        cp.wait_send()
    for k, cp in tnear:
        pl.when(jnp.logical_not(ends[k]))(cp.wait_send)
    pl.when(inner)(att_hop(far_seg, 3 - far_seg).wait_send)
    dq = dot3((phi[...], plo[...]), (khi[...], klo[...]), TN) * (1.0 / math.sqrt(HD))
    dqs[...] = dq.reshape(2, 128, HD)
    go(rcopy(dqs.at[1 - c], dq_ref.at[:, half_cols(c)], qos, qor, sq=q_sib))
    dq_ref[:, half_cols(c)] = dqs[c]
    sum_near(0)
    dw_end()
    sum_end(1)
    sum_end(0)
    rcopy(dqs.at[1 - c], dq_ref.at[:, half_cols(1 - c)], qos, qor, sq=q_sib).wait_recv()

    for cp in sends:
        cp.wait_send()
    for i in (0, 1, 3):
        ysend[i].wait_send()
    pl.when(other)(ysend[2].wait_send)

    @pl.when(odd == 0)
    def _():
        for n in range(8):
            zcopy(0, n, zo.at[n, 0], 1).wait_send()
            zcopy(0, n, zo.at[n, 1], -1).wait_send()

    @pl.when(odd == 1)
    def _():
        for n in range(8):
            zcopy(3, n, zs.at[n, 2], 1).wait_send()

    for n in range(8):
        for i in range(2):
            zcopy(3, n, zs.at[n, i], 1).wait_send()


def keep(*refs):
    sems = refs[8]
    copies = [pltpu.make_async_copy(refs[i], refs[4 + i], sems.at[i]) for i in range(4)]
    for cp in copies:
        cp.start()
    for cp in copies:
        cp.wait()


def shards(query, key_in, value, out_grad, w_out):
    blk = (128, 256)
    vmem = pl.BlockSpec(memory_space=pltpu.VMEM)
    hbm = pl.BlockSpec(memory_space=pltpu.HBM)
    sem = lambda *n: pltpu.SemaphoreType.DMA(n)
    one = pltpu.SemaphoreType.DMA
    f32 = lambda *n: pltpu.VMEM(n, F32)
    b16 = lambda *n: pltpu.VMEM(n, BF16)
    outs = pl.pallas_call(
        body,
        out_shape=[jax.ShapeDtypeStruct(blk, F32)] * 4,
        in_specs=[hbm] * 5,
        out_specs=[vmem] * 4,
        scratch_shapes=[
            f32(2, 128, 128),
            f32(2, 8, 128, 128),
            f32(8, 128, 256),
            f32(4, 4, 2, 128, 128),
            b16(4, 128, 1024), b16(4, 128, 1024),
            f32(4, 2, 128, 128),
            b16(4, 128, 256), b16(4, 128, 256),
            f32(4, 2, 128, 128),
            f32(4, 2, 128, 128),
            f32(2, 128, 128),
            f32(4, 2, 256, 128),
            f32(4, 256, 128),
            f32(4, 256, 128),
            f32(2, 128, 128),
            f32(2, 256, 128),
            f32(2, 4, 2, 128, 128),
            f32(2, 2, 2, 64, 128),
            f32(2, 2, 2, 128, 128),
            f32(2, 128, 128),
            b16(256, 128), b16(256, 128),
            b16(1024, 128), b16(1024, 128),
            b16(1024, 128), b16(1024, 128),
            b16(1024, 256), b16(1024, 256),
            f32(1024, 256),
            b16(1024, 256), b16(1024, 256),
            sem(5), one, one,
            sem(2, 4, 2), sem(2, 4, 2), sem(2), sem(2),
            sem(4), sem(4), sem(4), sem(4),
            sem(4), sem(4, 2),
            sem(8, 3), sem(8, 2), sem(8, 4),
            sem(4, 2), sem(4, 2), one, one, sem(4, 2), sem(4, 2),
            one, one, sem(6), sem(6),
            sem(2, 2), sem(2, 2),
            sem(2, 2, 2, 2), sem(2, 2, 2, 2),
            sem(2), sem(2), one, one,
        ],
        compiler_params=pltpu.CompilerParams(
            collective_id=0, has_side_effects=True, vmem_limit_bytes=60 * 1024 * 1024
        ),
        cost_estimate=pl.CostEstimate(
            flops=3 * 940_000_000, bytes_accessed=1_200_000, transcendentals=262_144
        ),
    )(query[0], key_in[0], value[0], out_grad[0], w_out)
    dq, dk, dv, dw = pl.pallas_call(
        keep,
        out_shape=[jax.ShapeDtypeStruct(blk, F32)] * 4,
        in_specs=[vmem] * 4,
        out_specs=[hbm] * 4,
        scratch_shapes=[sem(4)],
        compiler_params=pltpu.CompilerParams(vmem_limit_bytes=60 * 1024 * 1024),
    )(*outs)
    return dq[None], dk[None], dv[None], dw


def solution(mesh):
    act = P("sg", "sq", "tp")
    wsp = P(("sq", "sg"), "tp")
    return jax.shard_map(
        shards,
        mesh=mesh,
        in_specs=(act, act, act, act, wsp),
        out_specs=(act, act, act, wsp),
        check_vma=False,
    )
```

```python
import math

import jax
import jax.numpy as jnp
from jax import lax
from jax.experimental import pallas as pl
from jax.experimental.pallas import tpu as pltpu
from jax.sharding import PartitionSpec as P

HD = 128
F32 = jnp.float32
BF16 = jnp.bfloat16
NN = (((1,), (0,)), ((), ()))
NT = (((1,), (1,)), ((), ()))
TN = (((0,), (0,)), ((), ()))


def rcopy(src, dst, ssem, rsem, **dev):
    return pltpu.make_async_remote_copy(
        src_ref=src,
        dst_ref=dst,
        send_sem=ssem,
        recv_sem=rsem,
        device_id=dev,
        device_id_type=pl.DeviceIdType.MESH,
    )


def split(x):
    hi = x.astype(BF16)
    return hi, (x - hi.astype(F32)).astype(BF16)


def dot3(a, b, dims):
    d = lambda u, v: lax.dot_general(u, v, dims, preferred_element_type=F32)
    return d(a[0], b[0]) + (d(a[0], b[1]) + d(a[1], b[0]))


def body(
    q_ref, k_ref, v_ref, og_ref, w_ref,
    dq_ref, dk_ref, dv_ref, dw_ref,
    qh, kv, wb, ogb, oghi, oglo, att, ahi, alo, psend, dpart, relayed, dqs,
    wpart, wsib, wred, whalf, wfull, part, half, near_in, own_in,
    qhi, qlo, khi, klo, vhi, vlo, whi, wlo, pt, phi, plo,
    lin, qs_s, qs_r, kxs, kxr, kss, ksr, xs, xr, ss, sr, ys, yr, zs, zo, zr,
    ts, tr, tf_s, tf_r, ds, dr, rel_r, ws1, wr1, ws2, wr2, hs, hr, fs, fr, os, orr, qos, qor,
):
    t = lax.axis_index("tp")
    q = lax.axis_index("sq")
    s = lax.axis_index("sg")
    yh, z = lax.div(t, 8), lax.rem(t, 8)
    x, c = lax.div(q, 2), lax.rem(q, 2)
    par = lax.div(s, 2)
    odd = lax.rem(z + par, 2)
    ring = lambda d: yh * 8 + lax.rem(z + d + 8, 8)
    x_right, x_left, x_far = lax.rem(x + 1, 4), lax.rem(x + 3, 4), lax.rem(x + 2, 4)
    q_right, q_left, q_far, q_sib = x_right * 2 + c, x_left * 2 + c, x_far * 2 + c, x * 2 + 1 - c
    sibling = lambda b: b + 1 - 2 * c
    att_seg = lambda k: lax.rem(s + (2, 1, 3)[k], 4)
    inner = jnp.logical_and(s > 0, s < 3)
    order = (
        jnp.where(inner, lax.rem(s + 1, 4), 3 - s),
        jnp.where(inner, lax.rem(s + 3, 4), lax.rem(s + 2, 4)),
        jnp.where(inner, lax.rem(s + 2, 4), jnp.where(s == 0, 1, 2)),
        s,
    )
    seg_at = lambda k: order[k]
    half_cols = lambda i: pl.ds(pl.multiple_of(i * HD, HD), HD)
    up, low = pl.ds(0, 64), pl.ds(64, 64)
    wup, wlow = pl.ds(0, 128), pl.ds(128, 128)

    barrier = pltpu.get_barrier_semaphore()
    partners = []
    for d in range(4):
        partners.append({"tp": (1 - yh) * 8 + z, "sg": lax.rem(s + d, 4)})
        for core in range(2):
            if d > 0:
                partners.append({"sg": lax.rem(s + d, 4), "sq": x * 2 + core})
                if d != 2:
                    partners.append({"sq": lax.rem(x + d, 4) * 2 + core})
    partners += [{"tp": ring(1)}, {"tp": ring(-1)}, {"sq": q_sib}]
    for p in partners:
        pl.semaphore_signal(barrier, inc=1, device_id=p, device_id_type=pl.DeviceIdType.MESH)
    pl.semaphore_wait(barrier, len(partners))

    sends = []

    def go(copy):
        copy.start()
        sends.append(copy)

    zi_own = lax.div(z, 2)
    in_pair = lax.rem(z, 2) == par
    next_to = 1 - lax.rem(s, 2)

    def y_send(i, h, far):
        target = 2 * lax.rem(z, 2) + h
        y = jnp.where(jnp.abs(s - target) == 3, 1 - yh, yh)
        return rcopy(
            og_ref.at[:, half_cols(h)],
            ogb.at[zi_own, s, yh],
            ys.at[i],
            yr.at[s, yh],
            tp=(1 - y if far else y) * 8 + z,
            sg=target,
        )

    ysend = [
        y_send(0, next_to, False),
        y_send(1, 1 - next_to, False),
        y_send(2, jnp.where(in_pair, next_to, 1 - next_to), True),
        y_send(3, jnp.where(in_pair, 1 - next_to, next_to), True),
    ]
    other = jnp.logical_not(in_pair)
    ysend[0].start()
    pl.when(other)(ysend[1].start)

    og_mine = og_ref.at[:, half_cols(lax.rem(s, 2))]
    og_local = pltpu.make_async_copy(og_mine, ogb.at[zi_own, s, yh], lin.at[4])

    nearer = [jnp.where(jnp.abs(seg_at(k) - s) == 3, 1 - yh, yh) for k in range(3)]
    pieces = [(s, yh), (seg_at(0), nearer[0]), (seg_at(2), nearer[2]), (seg_at(0), 1 - nearer[0])]
    pieces += [(seg_at(1), nearer[1]), (seg_at(1), 1 - nearer[1]), (seg_at(2), 1 - nearer[2]), (s, 1 - yh)]

    def zcopy(d, n, sem, step):
        zi = lax.div(lax.rem(z - d + 16, 8), 2)
        j, y = pieces[n]
        ref = ogb.at[zi, j, y]
        src = og_mine if d == 0 and n == 0 else ref
        return rcopy(src, ref, sem, zr.at[n, zi], tp=ring(step))

    def own(n):
        if n > 0:
            j, y = pieces[n]
            blk = ogb.at[zi_own, j, y]
            rcopy(blk, blk, ys.at[0], yr.at[j, y], tp=t, sg=s).wait_recv()
        zcopy(0, n, zo.at[n, 0], 1).start()
        zcopy(0, n, zo.at[n, 1], -1).start()

    @pl.when(odd == 0)
    def _():
        own(0)
        og_local.start()

    kv_in = (k_ref, v_ref)
    for a in range(2):
        for side, xo in enumerate((x_right, x_left)):
            for core in range(2):
                go(rcopy(kv_in[a].at[:, pl.ds(core * HD, HD)], kv.at[a, q],
                         kxs.at[a, side, core], kxr.at[a, side, c], sq=xo * 2 + core))
        go(rcopy(kv_in[a].at[:, half_cols(1 - c)], kv.at[a, q], kss.at[a], ksr.at[a], sq=q_sib))
    go(rcopy(q_ref.at[:, half_cols(1 - c)], qh.at[c], qs_s, qs_r, sq=q_sib))
    local = [pltpu.make_async_copy(kv_in[a].at[:, half_cols(c)], kv.at[a, q], lin.at[a]) for a in range(2)]
    local.append(pltpu.make_async_copy(w_ref, wb.at[q], lin.at[2]))
    local.append(pltpu.make_async_copy(q_ref.at[:, half_cols(c)], qh.at[c], lin.at[3]))
    for cp in local:
        cp.start()
    ysend[0].wait_send()
    ysend[2].start()
    ysend[3].start()

    def kv_copy(a, side, core, xs_, xd, rows=None, hop=0):
        blk = kv.at[a, xs_ * 2 + core]
        if rows is not None:
            blk = kv.at[a, xs_ * 2 + core, rows]
        return rcopy(blk, blk, kxs.at[a, side + 2 * hop, core], kxr.at[a, side + 2 * hop, core], sq=xd * 2 + c)

    def kv_near(a):
        for side, (xs_, xd, rows) in enumerate(((x_left, x_right, up), (x_right, x_left, low))):
            for core in range(2):
                kv_copy(a, side, core, xs_, xd).wait_recv()
                go(kv_copy(a, side, core, xs_, xd, rows, 1))

    def kv_done(a):
        for core in range(2):
            kv_copy(a, 0, core, x_far, x_right, up, 1).wait_recv()
            kv_copy(a, 1, core, x_far, x_left, low, 1).wait_recv()
        rcopy(kv.at[a, q_sib], kv.at[a, q_sib], kss.at[a], ksr.at[a], sq=q_sib).wait_recv()
        local[a].wait()

    def w_start():
        go(rcopy(w_ref, wb.at[q], xs.at[0], xr.at[0], sq=q_right))
        go(rcopy(w_ref, wb.at[q], xs.at[1], xr.at[1], sq=q_left))
        go(rcopy(w_ref, wb.at[q], ss.at[0], sr.at[0], sq=q_sib))

    def w_near():
        blk = wb.at[q_left]
        rcopy(blk, blk, xs.at[0], xr.at[0], sq=q_right).wait_recv()
        hb = wb.at[q_left, up]
        go(rcopy(hb, hb, xs.at[2], xr.at[2], sq=q_right))
        go(rcopy(blk, blk, ss.at[1], sr.at[1], sq=q_sib))
        blk = wb.at[q_right]
        rcopy(blk, blk, xs.at[1], xr.at[1], sq=q_left).wait_recv()
        hb = wb.at[q_right, low]
        go(rcopy(hb, hb, xs.at[3], xr.at[3], sq=q_left))
        go(rcopy(blk, blk, ss.at[2], sr.at[2], sq=q_sib))

    def w_far():
        for i, rows in enumerate((up, low)):
            hb = wb.at[q_far, rows]
            rcopy(hb, hb, xs.at[2 + i], xr.at[2 + i], sq=q_right).wait_recv()
        blk = wb.at[q_far]
        go(rcopy(blk, blk, ss.at[3], sr.at[3], sq=q_sib))

    def w_done():
        for i, b in enumerate((q, q_left, q_right, q_far)):
            blk = wb.at[sibling(b)]
            rcopy(blk, blk, ss.at[i], sr.at[i], sq=q_sib).wait_recv()
        local[2].wait()
        for b in range(8):
            rows = pl.ds(b * 128, 128)
            whi[rows, :], wlo[rows, :] = split(wb[b])

    on_right, on_left = (1, 0, 2, 3, 5, 4, 7, 6), (0, 4, 1, 3, 5, 6, 2, 7)
    long_right = (1, 2, 5, 7)

    def pass_near(n, odd):
        right, left = (n, n) if odd else (on_right[n], on_left[n])
        cp = zcopy(2 - odd, right, zs.at[right, 0], 1)
        cp.wait_recv()
        cp.start()
        cp = zcopy(6 + odd, left, zs.at[left, 1], -1)
        cp.wait_recv()
        cp.start()

    def pass_far(n):
        cp = zcopy(3, n, zs.at[n, 2], 1) if n in long_right else zcopy(5, n, zs.at[n, 2], -1)
        cp.wait_recv()
        cp.start()

    def ring_steps(owns=(), near_even=(), near_odd=(), fars=()):
        @pl.when(odd == 0)
        def _():
            for n in owns:
                own(n)
            for n in near_even:
                pass_near(n, 0)

        @pl.when(odd == 1)
        def _():
            for n in near_odd:
                pass_near(n, 1)
            for n in fars:
                pass_far(n)

    def arrived(n):
        @pl.when(odd == 0)
        def _():
            zcopy(4, n, zs.at[n, 2], 1).wait_recv()

        @pl.when(odd == 1)
        def _():
            zcopy(5 if n in long_right else 3, n, zs.at[n, 2], 1).wait_recv()

    def og_pairs(k):
        j = seg_at(k)
        for zi in range(4):
            for y in range(2):
                hi, lo = split(ogb[zi, j, y])
                cols = pl.ds((y * 4 + zi) * HD, HD)
                oghi[k, :, cols] = hi
                oglo[k, :, cols] = lo

    def send_partial(k):
        return [
            rcopy(psend.at[k, core], dpart.at[s, c], ds.at[k, core], dr.at[s, c], sg=seg_at(k), sq=x * 2 + core)
            for core in range(2)
        ]

    def relay():
        return rcopy(psend.at[0], relayed, ds.at[3, 0], rel_r, sg=jnp.where(s < 2, 1, 2))

    def partial_dot(k):
        res = dot3((oghi[k], oglo[k]), (whi[...], wlo[...]), NN)
        psend[k, 0] = res[:, :HD]
        psend[k, 1] = res[:, HD:]
        if k == 0:
            pl.when(jnp.logical_not(inner))(relay().start)

            @pl.when(inner)
            def _():
                for cp in send_partial(0):
                    cp.start()
        elif k < 3:
            if k == 2:
                @pl.when(inner)
                def _():
                    rcopy(relayed, relayed, ds.at[3, 0], rel_r, sg=s, sq=q_sib).wait_recv()
                    psend[2] = psend[2] + relayed[...]
            for cp in send_partial(k):
                go(cp)
        else:
            go(rcopy(psend.at[3, 1 - c], dpart.at[s, c], ds.at[3, 1], dr.at[s, c], sq=q_sib))
            dpart[s, c] = psend[3, c]

            @pl.when(jnp.logical_not(inner))
            def _():
                dpart[3 - s] = jnp.zeros((2, 128, HD), F32)

    def probs():
        rcopy(qh.at[1 - c], qh.at[1 - c], qs_s, qs_r, sq=q_sib).wait_recv()
        local[3].wait()
        qhi[...], qlo[...] = split(qh[...].reshape(256, HD) * (1.0 / math.sqrt(HD)))
        kv_done(0)
        khi[...], klo[...] = split(kv[0].reshape(1024, HD))
        st = dot3((khi[...], klo[...]), (qhi[...], qlo[...]), NT)
        e = jnp.exp(st - jnp.max(st, axis=0, keepdims=True))
        p = e / jnp.sum(e, axis=0, keepdims=True)
        pt[...] = p
        phi[...], plo[...] = split(p)

    ends = (None, s == 3, s == 0)
    far_seg = jnp.where(s == 2, 0, 3)
    tsends, tnear = [], []

    def att_hop(j, to_seg):
        return rcopy(att.at[j], att.at[j], tf_s, tf_r, sg=to_seg)

    def att_forward():
        @pl.when(inner)
        def _():
            for head in range(2):
                blk = att.at[far_seg, head]
                rcopy(blk, blk, ts.at[0, 0], tr.at[0, head], sq=q_sib).wait_recv()
            att_hop(far_seg, 3 - far_seg).start()

    def to(copy):
        copy.start()
        tsends.append(copy)

    def attend():
        kv_done(1)
        vhi[...], vlo[...] = split(kv[1].reshape(1024, HD))
        res = dot3((phi[...], plo[...]), (vhi[...], vlo[...]), TN)
        dqs[...] = res.reshape(2, 128, HD)
        for k in range(3):
            for core in range(2):
                cp = rcopy(dqs.at[core], att.at[s, c], ts.at[k, core], tr.at[k, c], sg=att_seg(k), sq=x * 2 + core)
                if k == 0:
                    to(cp)
                else:
                    pl.when(jnp.logical_not(ends[k]))(cp.start)
                    tnear.append((k, cp))
        to(rcopy(dqs.at[1 - c], att.at[s, c], ts.at[3, 0], tr.at[3, c], sq=q_sib))
        att[s, c] = dqs[c]

    def att_arrived():
        for k in range(3):
            j = att_seg(k)
            k_from = (0, 2, 1)[k]

            def direct():
                for head in range(2):
                    blk = att.at[j, head]
                    rcopy(blk, blk, ts.at[k_from, 0], tr.at[k_from, head], sq=q_sib).wait_recv()

            if k == 0:
                pl.when(jnp.logical_not(inner))(direct)
            else:
                pl.when(jnp.logical_not(ends[k]))(direct)
                pl.when(ends[k])(att_hop(j, s).wait_recv)
        blk = att.at[s, 1 - c]
        rcopy(blk, blk, ts.at[3, 0], tr.at[3, 1 - c], sq=q_sib).wait_recv()

    def att_pairs(k):
        j = seg_at(k)
        for head in range(2):
            cols = pl.ds(head * HD, HD)
            ahi[k, :, cols], alo[k, :, cols] = split(att[j, head])

    def dw_add(k):
        att_pairs(k)
        att_pairs(k + 1)
        rows = pl.ds(k, 2)
        a = (ahi[rows].reshape(256, 256), alo[rows].reshape(256, 256))
        g = (oghi[rows].reshape(256, 1024), oglo[rows].reshape(256, 1024))
        dw = dot3(a, g, TN)
        for b in range(8):
            part_b = dw[:, b * 128:(b + 1) * 128]
            wpart[b // 2, b % 2] = part_b if k == 0 else wpart[b // 2, b % 2] + part_b

    ring_steps(owns=(1,), near_odd=(0,))
    kv_near(0)
    ring_steps(owns=(2, 4, 3), near_odd=(1,))
    kv_near(1)
    w_start()
    ring_steps(owns=(5, 6), near_odd=(2,))
    probs()
    ring_steps(owns=(7,), near_odd=(4, 3))
    attend()
    ring_steps(near_even=(0,), near_odd=(5,))
    w_near()
    ring_steps(near_even=(1, 2, 3), near_odd=(6, 7))
    w_far()
    ring_steps(near_even=(4,), fars=(0,))
    w_done()
    ring_steps(near_even=(5, 6, 7), fars=(1, 2, 4))
    att_forward()
    ring_steps(fars=(3,))
    arrived(1)
    arrived(3)
    og_pairs(0)
    partial_dot(0)
    ring_steps(fars=(5,))
    arrived(4)
    arrived(5)
    og_pairs(1)
    partial_dot(1)
    ring_steps(fars=(6, 7))
    arrived(2)
    arrived(6)
    og_pairs(2)
    partial_dot(2)
    att_arrived()
    dw_add(0)

    @pl.when(odd == 0)
    def _():
        og_local.wait()

    arrived(0)
    arrived(7)
    og_pairs(3)
    dw_add(2)
    go(rcopy(wpart.at[:, 1 - c], wsib, ws1, wr1, sq=q_sib))
    partial_dot(3)

    def dw_far():
        rcopy(wpart.at[:, 1 - c], wsib, ws1, wr1, sq=q_sib).wait_recv()
        wred[x_far] = wpart[x_far, c] + wsib[x_far]
        go(rcopy(wred.at[x_far, wup], whalf.at[0], ws2.at[0], wr2.at[0], sq=q_right))
        go(rcopy(wred.at[x_far, wlow], whalf.at[1], ws2.at[1], wr2.at[1], sq=q_left))
        wred[x_right] = wpart[x_right, c] + wsib[x_right]
        go(rcopy(wred.at[x_right, wlow], wfull.at[0, wlow], ws2.at[2], wr2.at[2], sq=q_right))
        wred[x_left] = wpart[x_left, c] + wsib[x_left]
        go(rcopy(wred.at[x_left, wup], wfull.at[1, wup], ws2.at[3], wr2.at[3], sq=q_left))
        wred[x] = wpart[x, c] + wsib[x]

    def dw_near():
        rcopy(whalf.at[0], whalf.at[0], ws2.at[0], wr2.at[0], sq=q_right).wait_recv()
        wred[x_right, wup] = wred[x_right, wup] + whalf[0]
        go(rcopy(wred.at[x_right, wup], wfull.at[0, wup], ws2.at[4], wr2.at[4], sq=q_right))
        rcopy(whalf.at[1], whalf.at[1], ws2.at[1], wr2.at[1], sq=q_left).wait_recv()
        wred[x_left, wlow] = wred[x_left, wlow] + whalf[1]
        go(rcopy(wred.at[x_left, wlow], wfull.at[1, wlow], ws2.at[5], wr2.at[5], sq=q_left))

    def dw_end():
        for i, (side, rows) in enumerate(((0, wlow), (1, wup), (0, wup), (1, wlow))):
            blk = wfull.at[side, rows]
            rcopy(blk, blk, ws2.at[2 + i], wr2.at[2 + i], sq=q_right).wait_recv()
        dw_ref[...] = (wred[x] + (wfull[0] + wfull[1])).T

    def near_rows(a, side, stage, xd, rows):
        for core in range(2):
            go(rcopy(part.at[a, xd, core, rows], near_in.at[a, side, c, rows],
                     fs.at[a, side, stage, core], fr.at[a, side, stage, c], sq=xd * 2 + core))

    def sum_start(a, right):
        def rows_of(xo):
            rows = pl.ds(pl.multiple_of(xo * 256, 256), 256)
            part[a, xo] = dot3((phi[rows, :], plo[rows, :]), right, NN).reshape(2, 128, HD)

        rows_of(x_far)
        go(rcopy(part.at[a, x_far, :, up], half.at[a, 0], hs.at[a, 0], hr.at[a, 0], sq=q_right))
        go(rcopy(part.at[a, x_far, :, low], half.at[a, 1], hs.at[a, 1], hr.at[a, 1], sq=q_left))
        rows_of(x_right)
        near_rows(a, 0, 0, x_right, low)
        rows_of(x_left)
        near_rows(a, 1, 0, x_left, up)
        rows_of(x)
        go(rcopy(part.at[a, x, 1 - c], own_in.at[a], os.at[a], orr.at[a], sq=q_sib))

    def sum_near(a):
        rcopy(half.at[a, 0], half.at[a, 0], hs.at[a, 0], hr.at[a, 0], sq=q_right).wait_recv()
        part[a, x_right, :, up] = part[a, x_right, :, up] + half[a, 0]
        near_rows(a, 0, 1, x_right, up)
        rcopy(half.at[a, 1], half.at[a, 1], hs.at[a, 1], hr.at[a, 1], sq=q_left).wait_recv()
        part[a, x_left, :, low] = part[a, x_left, :, low] + half[a, 1]
        near_rows(a, 1, 1, x_left, low)

    outs = (dk_ref, dv_ref)

    def sum_end(a):
        for side in range(2):
            for stage in range(2):
                rows = low if side == stage else up
                for core in range(2):
                    blk = near_in.at[a, side, core, rows]
                    rcopy(blk, blk, fs.at[a, side, stage, core], fr.at[a, side, stage, core], sq=q_right).wait_recv()
        rcopy(own_in.at[a], own_in.at[a], os.at[a], orr.at[a], sq=q_sib).wait_recv()
        outs[a][:, half_cols(c)] = part[a, x, c] + (near_in[a, 0, c] + near_in[a, 1, c])
        outs[a][:, half_cols(1 - c)] = own_in[a] + (near_in[a, 0, 1 - c] + near_in[a, 1, 1 - c])

    dw_far()
    for d in range(1, 4):
        src = lax.rem(s + d, 4)

        @pl.when(jnp.logical_or(inner, src != 3 - s))
        def _():
            for core in range(2):
                blk = dpart.at[src, core]
                rcopy(blk, blk, ds.at[0, 0], dr.at[src, core], sq=q_sib).wait_recv()
    blk = dpart.at[s, 1 - c]
    rcopy(blk, blk, ds.at[3, 1], dr.at[s, 1 - c], sq=q_sib).wait_recv()
    datt = ((dpart[0] + dpart[1]) + (dpart[2] + dpart[3])).reshape(256, HD)
    dsp = split(datt)
    sum_start(1, dsp)
    dp = dot3((vhi[...], vlo[...]), dsp, NT)
    p = pt[...]
    dsc = p * (dp - jnp.sum(p * dp, axis=0, keepdims=True))
    phi[...], plo[...] = split(dsc)
    sum_start(0, (qhi[...], qlo[...]))
    dw_near()
    sum_near(1)
    for cp in tsends:
        cp.wait_send()
    for k, cp in tnear:
        pl.when(jnp.logical_not(ends[k]))(cp.wait_send)
    pl.when(inner)(att_hop(far_seg, 3 - far_seg).wait_send)
    dq = dot3((phi[...], plo[...]), (khi[...], klo[...]), TN) * (1.0 / math.sqrt(HD))
    dqs[...] = dq.reshape(2, 128, HD)
    go(rcopy(dqs.at[1 - c], dq_ref.at[:, half_cols(c)], qos, qor, sq=q_sib))
    dq_ref[:, half_cols(c)] = dqs[c]
    sum_near(0)
    dw_end()
    sum_end(1)
    sum_end(0)
    rcopy(dqs.at[1 - c], dq_ref.at[:, half_cols(1 - c)], qos, qor, sq=q_sib).wait_recv()

    for cp in sends:
        cp.wait_send()
    pl.when(jnp.logical_not(inner))(relay().wait_send)

    @pl.when(inner)
    def _():
        for cp in send_partial(0):
            cp.wait_send()

    pl.when(other)(ysend[1].wait_send)
    ysend[2].wait_send()
    ysend[3].wait_send()

    @pl.when(odd == 0)
    def _():
        for n in range(8):
            zcopy(0, n, zo.at[n, 0], 1).wait_send()
            zcopy(0, n, zo.at[n, 1], -1).wait_send()

    @pl.when(odd == 1)
    def _():
        for n in range(8):
            zcopy(3, n, zs.at[n, 2], 1).wait_send()

    for n in range(8):
        for i in range(2):
            zcopy(3, n, zs.at[n, i], 1).wait_send()


def keep(*refs):
    sems = refs[8]
    copies = [pltpu.make_async_copy(refs[i], refs[4 + i], sems.at[i]) for i in range(4)]
    for cp in copies:
        cp.start()
    for cp in copies:
        cp.wait()


def shards(query, key_in, value, out_grad, w_out):
    blk = (128, 256)
    vmem = pl.BlockSpec(memory_space=pltpu.VMEM)
    hbm = pl.BlockSpec(memory_space=pltpu.HBM)
    sem = lambda *n: pltpu.SemaphoreType.DMA(n)
    one = pltpu.SemaphoreType.DMA
    f32 = lambda *n: pltpu.VMEM(n, F32)
    b16 = lambda *n: pltpu.VMEM(n, BF16)
    outs = pl.pallas_call(
        body,
        out_shape=[jax.ShapeDtypeStruct(blk, F32)] * 4,
        in_specs=[hbm] * 5,
        out_specs=[vmem] * 4,
        scratch_shapes=[
            f32(2, 128, 128),
            f32(2, 8, 128, 128),
            f32(8, 128, 256),
            f32(4, 4, 2, 128, 128),
            b16(4, 128, 1024), b16(4, 128, 1024),
            f32(4, 2, 128, 128),
            b16(4, 128, 256), b16(4, 128, 256),
            f32(4, 2, 128, 128),
            f32(4, 2, 128, 128),
            f32(2, 128, 128),
            f32(2, 128, 128),
            f32(4, 2, 256, 128),
            f32(4, 256, 128),
            f32(4, 256, 128),
            f32(2, 128, 128),
            f32(2, 256, 128),
            f32(2, 4, 2, 128, 128),
            f32(2, 2, 2, 64, 128),
            f32(2, 2, 2, 128, 128),
            f32(2, 128, 128),
            b16(256, 128), b16(256, 128),
            b16(1024, 128), b16(1024, 128),
            b16(1024, 128), b16(1024, 128),
            b16(1024, 256), b16(1024, 256),
            f32(1024, 256),
            b16(1024, 256), b16(1024, 256),
            sem(5), one, one,
            sem(2, 4, 2), sem(2, 4, 2), sem(2), sem(2),
            sem(4), sem(4), sem(4), sem(4),
            sem(4), sem(4, 2),
            sem(8, 3), sem(8, 2), sem(8, 4),
            sem(4, 2), sem(4, 2), one, one, sem(4, 2), sem(4, 2), one,
            one, one, sem(6), sem(6),
            sem(2, 2), sem(2, 2),
            sem(2, 2, 2, 2), sem(2, 2, 2, 2),
            sem(2), sem(2), one, one,
        ],
        compiler_params=pltpu.CompilerParams(
            collective_id=0, has_side_effects=True, vmem_limit_bytes=60 * 1024 * 1024
        ),
        cost_estimate=pl.CostEstimate(
            flops=3 * 940_000_000, bytes_accessed=1_200_000, transcendentals=262_144
        ),
    )(query[0], key_in[0], value[0], out_grad[0], w_out)
    dq, dk, dv, dw = pl.pallas_call(
        keep,
        out_shape=[jax.ShapeDtypeStruct(blk, F32)] * 4,
        in_specs=[vmem] * 4,
        out_specs=[hbm] * 4,
        scratch_shapes=[sem(4)],
        compiler_params=pltpu.CompilerParams(vmem_limit_bytes=60 * 1024 * 1024),
    )(*outs)
    return dq[None], dk[None], dv[None], dw


def solution(mesh):
    act = P("sg", "sq", "tp")
    wsp = P(("sq", "sg"), "tp")
    return jax.shard_map(
        shards,
        mesh=mesh,
        in_specs=(act, act, act, act, wsp),
        out_specs=(act, act, act, wsp),
        check_vma=False,
    )
```

```python
import math

import jax
import jax.numpy as jnp
from jax import lax
from jax.experimental import pallas as pl
from jax.experimental.pallas import tpu as pltpu
from jax.sharding import PartitionSpec as P

HD = 128
F32 = jnp.float32
BF16 = jnp.bfloat16
NN = (((1,), (0,)), ((), ()))
NT = (((1,), (1,)), ((), ()))
TN = (((0,), (0,)), ((), ()))


def rcopy(src, dst, ssem, rsem, **dev):
    return pltpu.make_async_remote_copy(
        src_ref=src,
        dst_ref=dst,
        send_sem=ssem,
        recv_sem=rsem,
        device_id=dev,
        device_id_type=pl.DeviceIdType.MESH,
    )


def split(x):
    hi = x.astype(BF16)
    return hi, (x - hi.astype(F32)).astype(BF16)


def dot3(a, b, dims):
    d = lambda u, v: lax.dot_general(u, v, dims, preferred_element_type=F32)
    return d(a[0], b[0]) + (d(a[0], b[1]) + d(a[1], b[0]))


def body(
    q_ref, k_ref, v_ref, og_ref, w_ref,
    dq_out, dk_out, dv_out, dw_out,
    dq_ref, dk_ref, dv_ref, dw_ref,
    qh, kv, wb, ogb, oghi, oglo, att, ahi, alo, psend, dpart, relayed, dqs,
    wpart, wsib, wred, whalf, wfull, part, half, near_in, own_in,
    qhi, qlo, khi, klo, vhi, vlo, whi, wlo, pt, phi, plo,
    lout, lin, qs_s, qs_r, kxs, kxr, kss, ksr, xs, xr, ss, sr, ys, yr, zs, zo, zr,
    ts, tr, tf_s, tf_r, ds, dr, rel_r, ws1, wr1, ws2, wr2, hs, hr, fs, fr, os, orr, qos, qor,
):
    t = lax.axis_index("tp")
    q = lax.axis_index("sq")
    s = lax.axis_index("sg")
    yh, z = lax.div(t, 8), lax.rem(t, 8)
    x, c = lax.div(q, 2), lax.rem(q, 2)
    par = lax.div(s, 2)
    odd = lax.rem(z + par, 2)
    ring = lambda d: yh * 8 + lax.rem(z + d + 8, 8)
    x_right, x_left, x_far = lax.rem(x + 1, 4), lax.rem(x + 3, 4), lax.rem(x + 2, 4)
    q_right, q_left, q_far, q_sib = x_right * 2 + c, x_left * 2 + c, x_far * 2 + c, x * 2 + 1 - c
    sibling = lambda b: b + 1 - 2 * c
    att_seg = lambda k: lax.rem(s + (2, 1, 3)[k], 4)
    inner = jnp.logical_and(s > 0, s < 3)
    order = (
        jnp.where(inner, lax.rem(s + 1, 4), 3 - s),
        jnp.where(inner, lax.rem(s + 3, 4), lax.rem(s + 2, 4)),
        jnp.where(inner, lax.rem(s + 2, 4), jnp.where(s == 0, 1, 2)),
        s,
    )
    seg_at = lambda k: order[k]
    half_cols = lambda i: pl.ds(pl.multiple_of(i * HD, HD), HD)
    up, low = pl.ds(0, 64), pl.ds(64, 64)
    wup, wlow = pl.ds(0, 128), pl.ds(128, 128)

    barrier = pltpu.get_barrier_semaphore()
    partners = []
    for d in range(4):
        partners.append({"tp": (1 - yh) * 8 + z, "sg": lax.rem(s + d, 4)})
        for core in range(2):
            if d > 0:
                partners.append({"sg": lax.rem(s + d, 4), "sq": x * 2 + core})
                if d != 2:
                    partners.append({"sq": lax.rem(x + d, 4) * 2 + core})
    partners += [{"tp": ring(1)}, {"tp": ring(-1)}, {"sq": q_sib}]
    for p in partners:
        pl.semaphore_signal(barrier, inc=1, device_id=p, device_id_type=pl.DeviceIdType.MESH)
    pl.semaphore_wait(barrier, len(partners))

    sends = []

    def go(copy):
        copy.start()
        sends.append(copy)

    zi_own = lax.div(z, 2)
    in_pair = lax.rem(z, 2) == par
    next_to = 1 - lax.rem(s, 2)

    def y_send(i, h, far):
        target = 2 * lax.rem(z, 2) + h
        y = jnp.where(jnp.abs(s - target) == 3, 1 - yh, yh)
        return rcopy(
            og_ref.at[:, half_cols(h)],
            ogb.at[zi_own, s, yh],
            ys.at[i],
            yr.at[s, yh],
            tp=(1 - y if far else y) * 8 + z,
            sg=target,
        )

    ysend = [
        y_send(0, next_to, False),
        y_send(1, 1 - next_to, False),
        y_send(2, jnp.where(in_pair, next_to, 1 - next_to), True),
        y_send(3, jnp.where(in_pair, 1 - next_to, next_to), True),
    ]
    other = jnp.logical_not(in_pair)
    ysend[0].start()
    pl.when(other)(ysend[1].start)

    og_mine = og_ref.at[:, half_cols(lax.rem(s, 2))]
    og_local = pltpu.make_async_copy(og_mine, ogb.at[zi_own, s, yh], lin.at[4])

    nearer = [jnp.where(jnp.abs(seg_at(k) - s) == 3, 1 - yh, yh) for k in range(3)]
    pieces = [(s, yh), (seg_at(0), nearer[0]), (seg_at(2), nearer[2]), (seg_at(0), 1 - nearer[0])]
    pieces += [(seg_at(1), nearer[1]), (seg_at(1), 1 - nearer[1]), (seg_at(2), 1 - nearer[2]), (s, 1 - yh)]

    def zcopy(d, n, sem, step):
        zi = lax.div(lax.rem(z - d + 16, 8), 2)
        j, y = pieces[n]
        ref = ogb.at[zi, j, y]
        src = og_mine if d == 0 and n == 0 else ref
        return rcopy(src, ref, sem, zr.at[n, zi], tp=ring(step))

    def own(n):
        if n > 0:
            j, y = pieces[n]
            blk = ogb.at[zi_own, j, y]
            rcopy(blk, blk, ys.at[0], yr.at[j, y], tp=t, sg=s).wait_recv()
        zcopy(0, n, zo.at[n, 0], 1).start()
        zcopy(0, n, zo.at[n, 1], -1).start()

    @pl.when(odd == 0)
    def _():
        own(0)
        og_local.start()

    kv_in = (k_ref, v_ref)
    for a in range(2):
        for side, xo in enumerate((x_right, x_left)):
            for core in range(2):
                go(rcopy(kv_in[a].at[:, pl.ds(core * HD, HD)], kv.at[a, q],
                         kxs.at[a, side, core], kxr.at[a, side, c], sq=xo * 2 + core))
        go(rcopy(kv_in[a].at[:, half_cols(1 - c)], kv.at[a, q], kss.at[a], ksr.at[a], sq=q_sib))
    go(rcopy(q_ref.at[:, half_cols(1 - c)], qh.at[c], qs_s, qs_r, sq=q_sib))
    local = [pltpu.make_async_copy(kv_in[a].at[:, half_cols(c)], kv.at[a, q], lin.at[a]) for a in range(2)]
    local.append(pltpu.make_async_copy(w_ref, wb.at[q], lin.at[2]))
    local.append(pltpu.make_async_copy(q_ref.at[:, half_cols(c)], qh.at[c], lin.at[3]))
    for cp in local:
        cp.start()
    ysend[0].wait_send()
    ysend[2].start()
    ysend[3].start()

    def kv_copy(a, side, core, xs_, xd, rows=None, hop=0):
        blk = kv.at[a, xs_ * 2 + core]
        if rows is not None:
            blk = kv.at[a, xs_ * 2 + core, rows]
        return rcopy(blk, blk, kxs.at[a, side + 2 * hop, core], kxr.at[a, side + 2 * hop, core], sq=xd * 2 + c)

    def kv_near(a):
        for side, (xs_, xd, rows) in enumerate(((x_left, x_right, up), (x_right, x_left, low))):
            for core in range(2):
                kv_copy(a, side, core, xs_, xd).wait_recv()
                go(kv_copy(a, side, core, xs_, xd, rows, 1))

    def kv_done(a):
        for core in range(2):
            kv_copy(a, 0, core, x_far, x_right, up, 1).wait_recv()
            kv_copy(a, 1, core, x_far, x_left, low, 1).wait_recv()
        rcopy(kv.at[a, q_sib], kv.at[a, q_sib], kss.at[a], ksr.at[a], sq=q_sib).wait_recv()
        local[a].wait()

    def w_start():
        go(rcopy(w_ref, wb.at[q], xs.at[0], xr.at[0], sq=q_right))
        go(rcopy(w_ref, wb.at[q], xs.at[1], xr.at[1], sq=q_left))
        go(rcopy(w_ref, wb.at[q], ss.at[0], sr.at[0], sq=q_sib))

    def w_near():
        blk = wb.at[q_left]
        rcopy(blk, blk, xs.at[0], xr.at[0], sq=q_right).wait_recv()
        hb = wb.at[q_left, up]
        go(rcopy(hb, hb, xs.at[2], xr.at[2], sq=q_right))
        go(rcopy(blk, blk, ss.at[1], sr.at[1], sq=q_sib))
        blk = wb.at[q_right]
        rcopy(blk, blk, xs.at[1], xr.at[1], sq=q_left).wait_recv()
        hb = wb.at[q_right, low]
        go(rcopy(hb, hb, xs.at[3], xr.at[3], sq=q_left))
        go(rcopy(blk, blk, ss.at[2], sr.at[2], sq=q_sib))

    def w_far():
        for i, rows in enumerate((up, low)):
            hb = wb.at[q_far, rows]
            rcopy(hb, hb, xs.at[2 + i], xr.at[2 + i], sq=q_right).wait_recv()
        blk = wb.at[q_far]
        go(rcopy(blk, blk, ss.at[3], sr.at[3], sq=q_sib))

    def w_done():
        for i, b in enumerate((q, q_left, q_right, q_far)):
            blk = wb.at[sibling(b)]
            rcopy(blk, blk, ss.at[i], sr.at[i], sq=q_sib).wait_recv()
        local[2].wait()
        for b in range(8):
            rows = pl.ds(b * 128, 128)
            whi[rows, :], wlo[rows, :] = split(wb[b])

    on_right, on_left = (1, 0, 2, 3, 5, 4, 7, 6), (0, 4, 1, 3, 5, 6, 2, 7)
    long_right = (1, 2, 5, 7)

    def pass_near(n, odd):
        right, left = (n, n) if odd else (on_right[n], on_left[n])
        cp = zcopy(2 - odd, right, zs.at[right, 0], 1)
        cp.wait_recv()
        cp.start()
        cp = zcopy(6 + odd, left, zs.at[left, 1], -1)
        cp.wait_recv()
        cp.start()

    def pass_far(n):
        cp = zcopy(3, n, zs.at[n, 2], 1) if n in long_right else zcopy(5, n, zs.at[n, 2], -1)
        cp.wait_recv()
        cp.start()

    def ring_steps(owns=(), near_even=(), near_odd=(), fars=()):
        @pl.when(odd == 0)
        def _():
            for n in owns:
                own(n)
            for n in near_even:
                pass_near(n, 0)

        @pl.when(odd == 1)
        def _():
            for n in near_odd:
                pass_near(n, 1)
            for n in fars:
                pass_far(n)

    def arrived(n):
        @pl.when(odd == 0)
        def _():
            zcopy(4, n, zs.at[n, 2], 1).wait_recv()

        @pl.when(odd == 1)
        def _():
            zcopy(5 if n in long_right else 3, n, zs.at[n, 2], 1).wait_recv()

    def og_pairs(k):
        j = seg_at(k)
        for zi in range(4):
            for y in range(2):
                hi, lo = split(ogb[zi, j, y])
                cols = pl.ds((y * 4 + zi) * HD, HD)
                oghi[k, :, cols] = hi
                oglo[k, :, cols] = lo

    def send_partial(k):
        return [
            rcopy(psend.at[k, core], dpart.at[s, c], ds.at[k, core], dr.at[s, c], sg=seg_at(k), sq=x * 2 + core)
            for core in range(2)
        ]

    def relay():
        return rcopy(psend.at[0], relayed, ds.at[3, 0], rel_r, sg=jnp.where(s < 2, 1, 2))

    def partial_dot(k):
        res = dot3((oghi[k], oglo[k]), (whi[...], wlo[...]), NN)
        psend[k, 0] = res[:, :HD]
        psend[k, 1] = res[:, HD:]
        if k == 0:
            pl.when(jnp.logical_not(inner))(relay().start)

            @pl.when(inner)
            def _():
                for cp in send_partial(0):
                    cp.start()
        elif k < 3:
            if k == 2:
                @pl.when(inner)
                def _():
                    rcopy(relayed, relayed, ds.at[3, 0], rel_r, sg=s, sq=q_sib).wait_recv()
                    psend[2] = psend[2] + relayed[...]
            for cp in send_partial(k):
                go(cp)
        else:
            go(rcopy(psend.at[3, 1 - c], dpart.at[s, c], ds.at[3, 1], dr.at[s, c], sq=q_sib))
            dpart[s, c] = psend[3, c]

            @pl.when(jnp.logical_not(inner))
            def _():
                dpart[3 - s] = jnp.zeros((2, 128, HD), F32)

    def probs():
        rcopy(qh.at[1 - c], qh.at[1 - c], qs_s, qs_r, sq=q_sib).wait_recv()
        local[3].wait()
        qhi[...], qlo[...] = split(qh[...].reshape(256, HD) * (1.0 / math.sqrt(HD)))
        kv_done(0)
        khi[...], klo[...] = split(kv[0].reshape(1024, HD))
        st = dot3((khi[...], klo[...]), (qhi[...], qlo[...]), NT)
        e = jnp.exp(st - jnp.max(st, axis=0, keepdims=True))
        p = e / jnp.sum(e, axis=0, keepdims=True)
        pt[...] = p
        phi[...], plo[...] = split(p)

    ends = (None, s == 3, s == 0)
    far_seg = jnp.where(s == 2, 0, 3)
    tsends, tnear = [], []

    def att_hop(j, to_seg):
        return rcopy(att.at[j], att.at[j], tf_s, tf_r, sg=to_seg)

    def att_forward():
        @pl.when(inner)
        def _():
            for head in range(2):
                blk = att.at[far_seg, head]
                rcopy(blk, blk, ts.at[0, 0], tr.at[0, head], sq=q_sib).wait_recv()
            att_hop(far_seg, 3 - far_seg).start()

    def to(copy):
        copy.start()
        tsends.append(copy)

    def attend():
        kv_done(1)
        vhi[...], vlo[...] = split(kv[1].reshape(1024, HD))
        res = dot3((phi[...], plo[...]), (vhi[...], vlo[...]), TN)
        dqs[...] = res.reshape(2, 128, HD)
        for k in range(3):
            for core in range(2):
                cp = rcopy(dqs.at[core], att.at[s, c], ts.at[k, core], tr.at[k, c], sg=att_seg(k), sq=x * 2 + core)
                if k == 0:
                    to(cp)
                else:
                    pl.when(jnp.logical_not(ends[k]))(cp.start)
                    tnear.append((k, cp))
        to(rcopy(dqs.at[1 - c], att.at[s, c], ts.at[3, 0], tr.at[3, c], sq=q_sib))
        att[s, c] = dqs[c]

    def att_arrived():
        for k in range(3):
            j = att_seg(k)
            k_from = (0, 2, 1)[k]

            def direct():
                for head in range(2):
                    blk = att.at[j, head]
                    rcopy(blk, blk, ts.at[k_from, 0], tr.at[k_from, head], sq=q_sib).wait_recv()

            if k == 0:
                pl.when(jnp.logical_not(inner))(direct)
            else:
                pl.when(jnp.logical_not(ends[k]))(direct)
                pl.when(ends[k])(att_hop(j, s).wait_recv)
        blk = att.at[s, 1 - c]
        rcopy(blk, blk, ts.at[3, 0], tr.at[3, 1 - c], sq=q_sib).wait_recv()

    def att_pairs(k):
        j = seg_at(k)
        for head in range(2):
            cols = pl.ds(head * HD, HD)
            ahi[k, :, cols], alo[k, :, cols] = split(att[j, head])

    def dw_swap(i, xo):
        return rcopy(wpart.at[xo, 1 - c], wsib.at[xo], ws1.at[i], wr1.at[i], sq=q_sib)

    def dw_add(k):
        att_pairs(k)
        att_pairs(k + 1)
        rows = pl.ds(k, 2)
        a = (ahi[rows].reshape(256, 256), alo[rows].reshape(256, 256))
        g = (oghi[rows].reshape(256, 1024), oglo[rows].reshape(256, 1024))
        dw = dot3(a, g, TN)
        for b in range(8):
            part_b = dw[:, b * 128:(b + 1) * 128]
            wpart[b // 2, b % 2] = part_b if k == 0 else wpart[b // 2, b % 2] + part_b

    ring_steps(owns=(1,), near_odd=(0,))
    kv_near(0)
    ring_steps(owns=(2, 4, 3), near_odd=(1,))
    kv_near(1)
    w_start()
    ring_steps(owns=(5, 6), near_odd=(2,))
    probs()
    ring_steps(owns=(7,), near_odd=(4, 3))
    attend()
    ring_steps(near_even=(0,), near_odd=(5,))
    w_near()
    ring_steps(near_even=(1, 2, 3), near_odd=(6, 7))
    w_far()
    ring_steps(near_even=(4,), fars=(0,))
    w_done()
    ring_steps(near_even=(5, 6, 7), fars=(1, 2, 4))
    att_forward()
    ring_steps(fars=(3,))
    arrived(1)
    arrived(3)
    og_pairs(0)
    partial_dot(0)
    ring_steps(fars=(5,))
    arrived(4)
    arrived(5)
    og_pairs(1)
    partial_dot(1)
    ring_steps(fars=(6, 7))
    arrived(2)
    arrived(6)
    og_pairs(2)
    partial_dot(2)
    att_arrived()
    dw_add(0)

    @pl.when(odd == 0)
    def _():
        og_local.wait()

    arrived(0)
    arrived(7)
    og_pairs(3)
    dw_add(2)
    for i, xo in enumerate((x_far, x_right, x_left, x)):
        go(dw_swap(i, xo))
    partial_dot(3)

    def dw_far():
        dw_swap(0, x_far).wait_recv()
        wred[x_far] = wpart[x_far, c] + wsib[x_far]
        go(rcopy(wred.at[x_far, wup], whalf.at[0], ws2.at[0], wr2.at[0], sq=q_right))
        go(rcopy(wred.at[x_far, wlow], whalf.at[1], ws2.at[1], wr2.at[1], sq=q_left))
        dw_swap(1, x_right).wait_recv()
        wred[x_right] = wpart[x_right, c] + wsib[x_right]
        go(rcopy(wred.at[x_right, wlow], wfull.at[0, wlow], ws2.at[2], wr2.at[2], sq=q_right))
        dw_swap(2, x_left).wait_recv()
        wred[x_left] = wpart[x_left, c] + wsib[x_left]
        go(rcopy(wred.at[x_left, wup], wfull.at[1, wup], ws2.at[3], wr2.at[3], sq=q_left))
        dw_swap(3, x).wait_recv()
        wred[x] = wpart[x, c] + wsib[x]

    def dw_near():
        rcopy(whalf.at[0], whalf.at[0], ws2.at[0], wr2.at[0], sq=q_right).wait_recv()
        wred[x_right, wup] = wred[x_right, wup] + whalf[0]
        go(rcopy(wred.at[x_right, wup], wfull.at[0, wup], ws2.at[4], wr2.at[4], sq=q_right))
        rcopy(whalf.at[1], whalf.at[1], ws2.at[1], wr2.at[1], sq=q_left).wait_recv()
        wred[x_left, wlow] = wred[x_left, wlow] + whalf[1]
        go(rcopy(wred.at[x_left, wlow], wfull.at[1, wlow], ws2.at[5], wr2.at[5], sq=q_left))

    def dw_end():
        for i, (side, rows) in enumerate(((0, wlow), (1, wup), (0, wup), (1, wlow))):
            blk = wfull.at[side, rows]
            rcopy(blk, blk, ws2.at[2 + i], wr2.at[2 + i], sq=q_right).wait_recv()
        dw_ref[...] = (wred[x] + (wfull[0] + wfull[1])).T

    def near_rows(a, side, stage, xd, rows):
        for core in range(2):
            go(rcopy(part.at[a, xd, core, rows], near_in.at[a, side, c, rows],
                     fs.at[a, side, stage, core], fr.at[a, side, stage, c], sq=xd * 2 + core))

    def sum_start(a, right):
        def rows_of(xo):
            rows = pl.ds(pl.multiple_of(xo * 256, 256), 256)
            part[a, xo] = dot3((phi[rows, :], plo[rows, :]), right, NN).reshape(2, 128, HD)

        rows_of(x_far)
        go(rcopy(part.at[a, x_far, :, up], half.at[a, 0], hs.at[a, 0], hr.at[a, 0], sq=q_right))
        go(rcopy(part.at[a, x_far, :, low], half.at[a, 1], hs.at[a, 1], hr.at[a, 1], sq=q_left))
        rows_of(x_right)
        near_rows(a, 0, 0, x_right, low)
        rows_of(x_left)
        near_rows(a, 1, 0, x_left, up)
        rows_of(x)
        go(rcopy(part.at[a, x, 1 - c], own_in.at[a], os.at[a], orr.at[a], sq=q_sib))

    def sum_near(a):
        rcopy(half.at[a, 0], half.at[a, 0], hs.at[a, 0], hr.at[a, 0], sq=q_right).wait_recv()
        part[a, x_right, :, up] = part[a, x_right, :, up] + half[a, 0]
        near_rows(a, 0, 1, x_right, up)
        rcopy(half.at[a, 1], half.at[a, 1], hs.at[a, 1], hr.at[a, 1], sq=q_left).wait_recv()
        part[a, x_left, :, low] = part[a, x_left, :, low] + half[a, 1]
        near_rows(a, 1, 1, x_left, low)

    outs = (dk_ref, dv_ref)

    def sum_end(a):
        for side in range(2):
            for stage in range(2):
                rows = low if side == stage else up
                for core in range(2):
                    blk = near_in.at[a, side, core, rows]
                    rcopy(blk, blk, fs.at[a, side, stage, core], fr.at[a, side, stage, core], sq=q_right).wait_recv()
        rcopy(own_in.at[a], own_in.at[a], os.at[a], orr.at[a], sq=q_sib).wait_recv()
        outs[a][:, half_cols(c)] = part[a, x, c] + (near_in[a, 0, c] + near_in[a, 1, c])
        outs[a][:, half_cols(1 - c)] = own_in[a] + (near_in[a, 0, 1 - c] + near_in[a, 1, 1 - c])

    dw_far()
    for d in range(1, 4):
        src = lax.rem(s + d, 4)

        @pl.when(jnp.logical_or(inner, src != 3 - s))
        def _():
            for core in range(2):
                blk = dpart.at[src, core]
                rcopy(blk, blk, ds.at[0, 0], dr.at[src, core], sq=q_sib).wait_recv()
    blk = dpart.at[s, 1 - c]
    rcopy(blk, blk, ds.at[3, 1], dr.at[s, 1 - c], sq=q_sib).wait_recv()
    datt = ((dpart[0] + dpart[1]) + (dpart[2] + dpart[3])).reshape(256, HD)
    dsp = split(datt)
    sum_start(1, dsp)
    dp = dot3((vhi[...], vlo[...]), dsp, NT)
    p = pt[...]
    dsc = p * (dp - jnp.sum(p * dp, axis=0, keepdims=True))
    phi[...], plo[...] = split(dsc)
    sum_start(0, (qhi[...], qlo[...]))
    dw_near()
    sum_near(1)
    for cp in tsends:
        cp.wait_send()
    for k, cp in tnear:
        pl.when(jnp.logical_not(ends[k]))(cp.wait_send)
    pl.when(inner)(att_hop(far_seg, 3 - far_seg).wait_send)
    dq = dot3((phi[...], plo[...]), (khi[...], klo[...]), TN) * (1.0 / math.sqrt(HD))
    dqs[...] = dq.reshape(2, 128, HD)
    go(rcopy(dqs.at[1 - c], dq_ref.at[:, half_cols(c)], qos, qor, sq=q_sib))
    dq_ref[:, half_cols(c)] = dqs[c]
    sum_near(0)
    results = [
        pltpu.make_async_copy(a, b, lout.at[i])
        for i, (a, b) in enumerate(((dq_ref, dq_out), (dk_ref, dk_out), (dv_ref, dv_out), (dw_ref, dw_out)))
    ]
    dw_end()
    results[3].start()
    sum_end(1)
    results[2].start()
    rcopy(dqs.at[1 - c], dq_ref.at[:, half_cols(1 - c)], qos, qor, sq=q_sib).wait_recv()
    results[0].start()
    sum_end(0)
    results[1].start()

    for cp in sends:
        cp.wait_send()
    pl.when(jnp.logical_not(inner))(relay().wait_send)

    @pl.when(inner)
    def _():
        for cp in send_partial(0):
            cp.wait_send()

    for cp in results:
        cp.wait()
    pl.when(other)(ysend[1].wait_send)
    ysend[2].wait_send()
    ysend[3].wait_send()

    @pl.when(odd == 0)
    def _():
        for n in range(8):
            zcopy(0, n, zo.at[n, 0], 1).wait_send()
            zcopy(0, n, zo.at[n, 1], -1).wait_send()

    @pl.when(odd == 1)
    def _():
        for n in range(8):
            zcopy(3, n, zs.at[n, 2], 1).wait_send()

    for n in range(8):
        for i in range(2):
            zcopy(3, n, zs.at[n, i], 1).wait_send()


def keep(*refs):
    held, in_sems, out_sems = refs[8:]
    rows = 128 // 4
    places = [(i, pl.ds(r * rows, rows)) for r in range(4) for i in range(4)]
    ins = [pltpu.make_async_copy(refs[i].at[r], held.at[i, r], in_sems.at[n]) for n, (i, r) in enumerate(places)]
    outs = [pltpu.make_async_copy(held.at[i, r], refs[4 + i].at[r], out_sems.at[n]) for n, (i, r) in enumerate(places)]
    for cp in ins:
        cp.start()
    for arriving, leaving in zip(ins, outs):
        arriving.wait()
        leaving.start()
    for cp in outs:
        cp.wait()


def shards(query, key_in, value, out_grad, w_out):
    blk = (128, 256)
    vmem = pl.BlockSpec(memory_space=pltpu.VMEM)
    hbm = pl.BlockSpec(memory_space=pltpu.HBM)
    sem = lambda *n: pltpu.SemaphoreType.DMA(n)
    one = pltpu.SemaphoreType.DMA
    f32 = lambda *n: pltpu.VMEM(n, F32)
    b16 = lambda *n: pltpu.VMEM(n, BF16)
    outs = pl.pallas_call(
        body,
        out_shape=[jax.ShapeDtypeStruct(blk, F32)] * 4,
        in_specs=[hbm] * 5,
        out_specs=[hbm] * 4,
        scratch_shapes=[
            f32(128, 256), f32(128, 256), f32(128, 256), f32(128, 256),
            f32(2, 128, 128),
            f32(2, 8, 128, 128),
            f32(8, 128, 256),
            f32(4, 4, 2, 128, 128),
            b16(4, 128, 1024), b16(4, 128, 1024),
            f32(4, 2, 128, 128),
            b16(4, 128, 256), b16(4, 128, 256),
            f32(4, 2, 128, 128),
            f32(4, 2, 128, 128),
            f32(2, 128, 128),
            f32(2, 128, 128),
            f32(4, 2, 256, 128),
            f32(4, 256, 128),
            f32(4, 256, 128),
            f32(2, 128, 128),
            f32(2, 256, 128),
            f32(2, 4, 2, 128, 128),
            f32(2, 2, 2, 64, 128),
            f32(2, 2, 2, 128, 128),
            f32(2, 128, 128),
            b16(256, 128), b16(256, 128),
            b16(1024, 128), b16(1024, 128),
            b16(1024, 128), b16(1024, 128),
            b16(1024, 256), b16(1024, 256),
            f32(1024, 256),
            b16(1024, 256), b16(1024, 256),
            sem(4), sem(5), one, one,
            sem(2, 4, 2), sem(2, 4, 2), sem(2), sem(2),
            sem(4), sem(4), sem(4), sem(4),
            sem(4), sem(4, 2),
            sem(8, 3), sem(8, 2), sem(8, 4),
            sem(4, 2), sem(4, 2), one, one, sem(4, 2), sem(4, 2), one,
            sem(4), sem(4), sem(6), sem(6),
            sem(2, 2), sem(2, 2),
            sem(2, 2, 2, 2), sem(2, 2, 2, 2),
            sem(2), sem(2), one, one,
        ],
        compiler_params=pltpu.CompilerParams(
            collective_id=0, has_side_effects=True, vmem_limit_bytes=60 * 1024 * 1024
        ),
        cost_estimate=pl.CostEstimate(
            flops=3 * 940_000_000, bytes_accessed=1_200_000, transcendentals=262_144
        ),
    )(query[0], key_in[0], value[0], out_grad[0], w_out)
    dq, dk, dv, dw = pl.pallas_call(
        keep,
        out_shape=[jax.ShapeDtypeStruct(blk, F32)] * 4,
        in_specs=[hbm] * 4,
        out_specs=[hbm] * 4,
        scratch_shapes=[f32(4, 128, 256), sem(16), sem(16)],
        compiler_params=pltpu.CompilerParams(vmem_limit_bytes=60 * 1024 * 1024),
    )(*outs)
    return dq[None], dk[None], dv[None], dw


def solution(mesh):
    act = P("sg", "sq", "tp")
    wsp = P(("sq", "sg"), "tp")
    return jax.shard_map(
        shards,
        mesh=mesh,
        in_specs=(act, act, act, act, wsp),
        out_specs=(act, act, act, wsp),
        check_vma=False,
    )
```
